128 devices in a mesh: sec: 2 (over z_lo), gx: 8 (over x, core), gy: 8 (over z_hi, y).
Axes of the slice: x: 4, y: 4, z: 4 (z_hi: 2, z_lo: 2; z = z_hi * 2 + z_lo), core: 2. Of those that a mesh axis runs over, the one named last changes fastest.
Arguments:
- state: float32 [4, 16, 1280, 2560], P(None, None, ('gx', 'gy'), 'sec'), may hold values from -6 to 6
- h_coeff: float32 [4, 16], replicated, may hold values from 0.03 to 0.12
- v_coeff: float32 [4, 16], replicated, may hold values from 0.03 to 0.15
- conv_weight: bfloat16 [4, 5, 5, 32], replicated, may hold values from -0.625 to 0.625
- conv_bias: float32 [32], replicated, may hold values from -3 to 3
- readout: float32 [32, 2], replicated, may hold values from -1 to 1
- readout_bias: float32 [2], replicated, may hold values from -2 to 2
- level_base: int32 [2, 256, 512], P(None, 'gx', ('sec', 'gy')), may hold values from 0 to 7
- level_depth: int32 [2, 256, 512], P(None, 'gx', ('sec', 'gy')), may hold values from 1 to 8
Outputs:
- advanced: float32 [4, 16, 1280, 2560], P(None, None, ('gx', 'gy'), 'sec')
- column_fraction: float32 [2, 256, 512], P(None, 'gx', ('sec', 'gy'))
- area_fraction: float32 [2, 256, 512], P(None, 'gx', ('sec', 'gy'))
The draws below stay inside these ranges and needn't reach their ends.
All inputs are finite; a program needn't handle non-finite values.
Results may differ from the reference program's by a relative error of at most 0.00033.
Values may be sent and summed in bfloat16 or wider, within the bound.
A program may use at most 384 MiB of HBM per device.

```python
import math
import jax
import jax.numpy as jnp
from jax import lax

FIELDS = 4
KERNEL = 5
CHANNELS = 32
WIN = 24
LEV = 16
NX = 1280
NY = 2560
NXC = 256
NYC = 512


def place_ends(values, key, low, top_value):
    index_at = [jax.random.randint(jax.random.fold_in(key, axis), (), 0, length) for axis, length in enumerate(values.shape)]
    widest = values.shape.index(max(values.shape))
    next_to = index_at[:widest] + [(index_at[widest] + 1) % values.shape[widest]] + index_at[widest + 1:]
    return values.at[tuple(index_at)].set(low).at[tuple(next_to)].set(top_value)


def block_levels(key, shape, pieces, least, top_value):
    loudness = 1.0
    for axis_at, parts in pieces:
        heights = jax.random.uniform(jax.random.fold_in(jax.random.fold_in(key, 6), axis_at), (parts,), jnp.float32, least / len(pieces), top_value / len(pieces))
        loudness = loudness * jnp.repeat(jnp.exp(heights), shape[axis_at] // parts).reshape((-1,) + (1,) * (len(shape) - 1 - axis_at))
    return loudness


def gaussian(rng, dims, scale, bound, pieces=(), held_as=jnp.bfloat16):
    gain = block_levels(rng, dims, pieces, -0.22, 0.18) if pieces else 1.0
    drawn = jax.random.normal(rng, dims, jnp.float32) * scale * gain
    return jnp.minimum(jnp.maximum(drawn, -bound), bound).astype(held_as)


def setup_inputs(seed: int = 0) -> dict:
    arg_keys = jax.random.split(jax.random.key(seed), 10)
    return {
        "state": gaussian(arg_keys[0], (FIELDS, LEV, NX, NY), 1.0, 6.0, ((2, 64), (3, 2)), jnp.float32),
        "h_coeff": jnp.clip(jnp.exp(jax.random.uniform(arg_keys[1], (FIELDS, LEV), jnp.float32, math.log(0.03), math.log(0.12))), 0.03, 0.12),
        "v_coeff": jnp.clip(jnp.exp(jax.random.uniform(arg_keys[2], (FIELDS, LEV), jnp.float32, math.log(0.03), math.log(0.15))), 0.03, 0.15),
        "conv_weight": gaussian(arg_keys[3], (FIELDS, KERNEL, KERNEL, CHANNELS), (FIELDS * KERNEL * KERNEL) ** -0.5, 0.625),
        "conv_bias": gaussian(arg_keys[4], (CHANNELS,), 0.5, 3.0, (), jnp.float32),
        "readout": gaussian(arg_keys[5], (CHANNELS, 2), CHANNELS ** -0.5, 1.0, (), jnp.float32),
        "readout_bias": jnp.clip(jax.random.uniform(arg_keys[6], (2,), jnp.float32, -2.0, 2.0), -2.0, 2.0),
        "level_base": place_ends(jax.random.randint(arg_keys[7], (2, NXC, NYC), 0, LEV // 2), jax.random.fold_in(arg_keys[7], 1), 0, (LEV // 2) - 1).astype(jnp.int32),
        "level_depth": place_ends(jax.random.randint(arg_keys[8], (2, NXC, NYC), 1, LEV // 2 + 1), jax.random.fold_in(arg_keys[8], 1), 1, (LEV // 2 + 1) - 1).astype(jnp.int32),
    }


def fourth_axis(field, axis):
    near = jnp.roll(field, 1, axis) + jnp.roll(field, -1, axis)
    far = jnp.roll(field, 2, axis) + jnp.roll(field, -2, axis)
    return (16.0 * near - far - 30.0 * field) / 12.0


def advance(field, horiz, vertical):
    laplace = fourth_axis(field, 1) + fourth_axis(field, 2)
    padded = jnp.pad(field, ((1, 1), (0, 0), (0, 0)))
    vert = padded[2:] + padded[:-2] - 2.0 * field
    return field + horiz[:, None, None] * laplace + vertical[:, None, None] * vert


def one_field(inputs):
    field, horiz, vertical = inputs
    return advance(advance(field, horiz, vertical), horiz, vertical)


def reference(state, h_coeff, v_coeff, conv_weight, conv_bias, readout, readout_bias, level_base, level_depth):
    advanced = lax.map(one_field, (state, h_coeff, v_coeff))
    kernel = conv_weight.astype(jnp.float32)
    top = level_base + level_depth

    def level_step(total, level):
        fields = lax.dynamic_index_in_dim(advanced, level, axis=1, keepdims=False)
        rounded = fields.astype(jnp.bfloat16).astype(jnp.float32)
        blocks = rounded.reshape(FIELDS, NXC, KERNEL, NYC, KERNEL)
        feats = jnp.einsum('fpaqb,fabk->pqk', blocks, kernel) + conv_bias
        feats = jnp.maximum(feats, 0.0)
        score = jnp.einsum('pqk,kc->cpq', feats, readout, precision=lax.Precision.HIGHEST)
        prob = jax.nn.sigmoid(score + readout_bias[:, None, None])
        inside = (level >= level_base) & (level < top)
        return total + jnp.where(inside, prob, 0.0), None

    total, _ = lax.scan(level_step, jnp.zeros((2, NXC, NYC), jnp.float32), jnp.arange(LEV, dtype=jnp.int32))
    column_fraction = total / level_depth.astype(jnp.float32)
    half = WIN // 2
    padded = jnp.pad(column_fraction, ((0, 0), (half, half), (half, half)), mode='wrap')
    rows = padded[:, 0:NXC, :]
    for shift in range(1, WIN):
        rows = rows + padded[:, shift:shift + NXC, :]
    window = rows[:, :, 0:NYC]
    for shift in range(1, WIN):
        window = window + rows[:, :, shift:shift + NYC]
    area_fraction = window / float(WIN * WIN)
    return advanced, column_fraction, area_fraction
```

```python
import jax
import jax.numpy as jnp
from jax import lax
from jax.experimental import pallas as pl
from jax.experimental.pallas import tpu as pltpu
from jax.sharding import PartitionSpec as P

F32 = jnp.float32
BF16 = jnp.bfloat16
MESH = pl.DeviceIdType.MESH

FIELDS = 4
LEV = 16
ROWS = 20
COLS = 1280
TILE = 128
TILES = COLS // TILE
WIDE = COLS + TILE
KERNEL = 5
CHANNELS = 32
COARSE = 256
WIN = 24
HALF = WIN // 2
GY = 8
GX = 8
SLOTS = 14


def lanes(shape):
    return lax.broadcasted_iota(jnp.int32, shape, len(shape) - 1)


def sublanes(shape):
    return lax.broadcasted_iota(jnp.int32, shape, len(shape) - 2)


def stencil_row(src, coef, f, r, count, emit):
    lane = lanes((8, TILE))
    sub = sublanes((8, TILE))
    rolled = {}

    def at(row, half, t):
        return src[f, row, 8 * half : 8 * half + 8, TILE * t : TILE * t + TILE]

    def roll(half, t, shift):
        t = t % (TILES + 1)
        key = (half, t, shift)
        if key not in rolled:
            rolled[key] = pltpu.roll(at(r, half, t), shift % TILE, 1)
        return rolled[key]

    c0, c1, c2, cv = (
        [coef[f, k, 8 * half : 8 * half + 8, :] for half in range(2)] for k in range(4)
    )
    for t in range(count):
        rolled = {k: v for k, v in rolled.items() if k[1] in (t - 1, t, t + 1) or (t == 0)}
        center = [at(r, half, t) for half in range(2)]
        down = [pltpu.roll(v, 1, 0) for v in center]
        up = [pltpu.roll(v, 7, 0) for v in center]
        vert = [
            jnp.where(sub == 0, 0.0, down[0]) + jnp.where(sub == 7, up[1], up[0]),
            jnp.where(sub == 0, down[0], down[1]) + jnp.where(sub == 7, 0.0, up[1]),
        ]
        for half in range(2):
            near = (at(r - 1, half, t) + at(r + 1, half, t)) + (
                jnp.where(lane < TILE - 1, roll(half, t, -1), roll(half, t + 1, -1))
                + jnp.where(lane < 1, roll(half, t - 1, 1), roll(half, t, 1))
            )
            far = (at(r - 2, half, t) + at(r + 2, half, t)) + (
                jnp.where(lane < TILE - 2, roll(half, t, -2), roll(half, t + 1, -2))
                + jnp.where(lane < 2, roll(half, t - 1, 2), roll(half, t, 2))
            )
            emit(
                half,
                t,
                (c0[half] * center[half] + c1[half] * near)
                + (c2[half] * far + cv[half] * vert[half]),
            )


def kernel(
    state,
    h_coeff,
    v_coeff,
    weight,
    conv_bias,
    readout,
    readout_bias,
    level_base,
    level_depth,
    out,
    column_out,
    area_out,
    st,
    u,
    adv,
    ab,
    coef,
    send_x,
    recv_x,
    send_p,
    recv_p,
    send_l,
    recv_l,
    select,
    conv_l,
    dmat,
    feat,
    cf,
    frac,
    load_sem,
    store_sem,
    sx_sem,
    rx_sem,
    sp_sem,
    rp_sem,
    sl_sem,
    rl_sem,
    sf_sem,
    rf_sem,
):
    sec, gx, gy = lax.axis_index("sec"), lax.axis_index("gx"), lax.axis_index("gy")
    other = 1 - sec
    gx_low, gx_high = lax.rem(gx + GX - 1, GX), lax.rem(gx + 1, GX)
    brick = gx * GY + gy
    low, high = lax.rem(brick + GX * GY - 1, GX * GY), lax.rem(brick + 1, GX * GY)
    low_x, low_y, high_x, high_y = low // GY, lax.rem(low, GY), high // GY, lax.rem(high, GY)
    near_low, near_high = gy <= 2, gy >= 5
    near_edge = near_low | near_high
    at_end = (gy == 0) | (gy == GY - 1)

    spans = ((0, 4), (16, 4), (4, 12))
    loads = []
    for part, (first, count) in enumerate(spans):
        for f in range(FIELDS):
            copy = pltpu.make_async_copy(
                state.at[f, pl.ds(first, count)],
                st.at[f, pl.ds(first + 4, count), :, pl.ds(0, COLS)],
                load_sem.at[part, f],
            )
            copy.start()
            loads.append(copy)

    barrier = pltpu.get_barrier_semaphore()

    def hello(where):
        pl.semaphore_signal(barrier, inc=1, device_id=where, device_id_type=MESH)

    hello((sec, low_x, low_y))
    hello((sec, high_x, high_y))
    hello((other, gx, gy))
    hello((other, low_x, low_y))
    hello((other, high_x, high_y))
    for k in range(1, GY):
        hello((sec, gx, lax.rem(gy + k, GY)))
    for k in range(3):
        hello((sec, gx_high, k))
        hello((sec, gx_low, 5 + k))

    @pl.when(at_end)
    def _():
        for k in range(GY):
            hello((other, gx, k))
        for k in range(3):
            hello((other, gx_high, k))
            hello((other, gx_low, 5 + k))

    eye = (sublanes((LEV, LEV)) == lanes((LEV, LEV))).astype(F32)
    for f in range(FIELDS):
        horiz = jnp.sum(eye * h_coeff[f : f + 1, :], axis=1, keepdims=True)
        vertical = jnp.sum(eye * v_coeff[f : f + 1, :], axis=1, keepdims=True)
        for k, value in enumerate(
            (
                1.0 - 5.0 * horiz - 2.0 * vertical,
                horiz * (16.0 / 12.0),
                horiz * (-1.0 / 12.0),
                vertical,
            )
        ):
            coef[f, k] = jnp.broadcast_to(value, (LEV, TILE))

    for copy in loads[: 2 * FIELDS]:
        copy.wait()

    lane = lanes((LEV, TILE))
    group_of = lax.rem(lane + 4, TILE) // 8

    @pl.loop(0, FIELDS)
    def _(f):
        for side, first in enumerate((4, 20)):
            for row in range(4):
                send_x[side, f, row] = st[f, first + row, :, :COLS].astype(BF16)

    def edge(f, row):
        return jnp.where(lane < 64, st[f, row, :, :TILE], st[f, row, :, COLS - TILE : COLS])

    def pack(group):
        total = jnp.zeros((LEV, TILE), F32)
        for j in range(16):
            part = pltpu.roll(edge(j // 4, 4 + 4 * group + j % 4), 8 * j, 1)
            total = jnp.where(group_of == j, part, total)
        send_p[group] = total

    pack(0)
    pack(4)

    send_l[...] = jnp.zeros_like(send_l)
    for k in range(GY):
        for c in range(2):
            for kind, ref in enumerate((level_base, level_depth)):
                send_l[k, kind, 4 * c : 4 * c + 4, 0:32] = ref[c, 4 * k : 4 * k + 4, :].astype(F32)
    turn = 32 * lax.rem(gy, 4)
    for k in range(GY):
        for kind in range(2):
            send_l[k, kind] = pltpu.roll(send_l[k, kind], turn, 1)

    for copy in loads[2 * FIELDS :]:
        copy.wait()
    for group in range(1, 4):
        pack(group)

    pl.semaphore_wait(barrier, 14 + jnp.where(near_edge, 10, 0))

    def copy_x(side, f):
        where = (sec, low_x, low_y) if side == 0 else (sec, high_x, high_y)
        return pltpu.make_async_remote_copy(
            send_x.at[side, f],
            recv_x.at[1 - side, f],
            sx_sem.at[side, f],
            rx_sem.at[1 - side, f],
            device_id=where,
            device_id_type=MESH,
        )

    def copy_p(k):
        source, target, where = (
            (send_p, recv_p.at[pl.ds(1, 5)], (other, gx, gy)),
            (send_p.at[0:1], recv_p.at[pl.ds(6, 1)], (other, low_x, low_y)),
            (send_p.at[4:5], recv_p.at[pl.ds(0, 1)], (other, high_x, high_y)),
        )[k]
        return pltpu.make_async_remote_copy(
            source, target, sp_sem.at[k], rp_sem.at[k], device_id=where, device_id_type=MESH
        )

    def copy_l(k):
        to = lax.rem(gy + k, GY)
        return pltpu.make_async_remote_copy(
            send_l.at[to],
            recv_l.at[gy],
            sl_sem.at[k],
            rl_sem.at[gy],
            device_id=(sec, gx, to),
            device_id_type=MESH,
        )

    copy_p(0).start()
    copy_x(0, 0).start()
    copy_x(1, 0).start()
    copy_p(1).start()
    copy_p(2).start()
    for f in range(1, FIELDS):
        copy_x(0, f).start()
        copy_x(1, f).start()
    for k in range(1, GY):
        copy_l(k).start()
    recv_l[gy] = send_l[gy]

    row = sublanes((KERNEL * TILE, TILE))
    col = lanes((KERNEL * TILE, TILE))
    for b in range(KERNEL):
        select[:, TILE * b : TILE * b + TILE] = (row == KERNEL * col + b).astype(F32).astype(BF16)
    spread = (
        sublanes((CHANNELS * LEV, CHANNELS)) // LEV == lanes((CHANNELS * LEV, CHANNELS))
    ).astype(F32).astype(BF16)
    wide_w = lax.dot_general(
        spread, weight[...], (((1,), (1,)), ((), ())), preferred_element_type=F32
    ).astype(BF16)
    taps = KERNEL * KERNEL
    for f in range(FIELDS):
        pick = (
            sublanes((taps * FIELDS, taps * LEV))
            == (lanes((taps * FIELDS, taps * LEV)) // LEV) * FIELDS + f
        ).astype(F32).astype(BF16)
        full = jnp.dot(wide_w, pick, preferred_element_type=F32)
        shape = (CHANNELS * LEV, taps * LEV)
        same = lax.rem(sublanes(shape), LEV) == lax.rem(lanes(shape), LEV)
        conv_l[f] = jnp.where(same, full, 0.0).astype(BF16)

    for k in range(3):
        copy_p(k).wait_recv()

    @pl.loop(0, 7)
    def _(group):
        for j in range(16):
            st[j // 4, 4 * group + j % 4, :, COLS:] = pltpu.roll(
                recv_p[group], (TILE - 8 * j) % TILE, 1
            )

    def first_step(f, r):
        def emit(half, t, value):
            u[f, r - 2, 8 * half : 8 * half + 8, TILE * t : TILE * t + TILE] = value

        stencil_row(st, coef, f, r, TILES + 1, emit)

    def second_step(f, r):
        kept = {}

        def emit(half, t, value):
            adv[f, r - 2, 8 * half : 8 * half + 8, TILE * t : TILE * t + TILE] = value
            kept[half, t] = value
            if half == 1:
                both = jnp.concatenate([kept.pop((0, t)), kept.pop((1, t))], axis=0)
                ab[f, r - 2, :, TILE * t : TILE * t + TILE] = both.astype(BF16)

        stencil_row(u, coef, f, r, TILES, emit)

    def store(part, f):
        first, count = spans[part]
        return pltpu.make_async_copy(
            adv.at[f, pl.ds(first, count)], out.at[f, pl.ds(first, count)], store_sem.at[part, f]
        )

    @pl.loop(0, FIELDS)
    def _(f):
        @pl.loop(6, 22)
        def _(r):
            first_step(f, r)

        @pl.loop(6, 18)
        def _(r):
            second_step(f, r)

        store(2, f).start()

    def convolve(f, p):
        for half in range(2):
            block = ab[f, KERNEL * p : KERNEL * p + KERNEL, :, 640 * half : 640 * half + 640]
            taken = jnp.dot(
                block.reshape(KERNEL * LEV, KERNEL * TILE), select[...], preferred_element_type=F32
            ).astype(BF16)
            for a in range(KERNEL):
                for b in range(KERNEL):
                    tap = LEV * (KERNEL * a + b)
                    dmat[tap : tap + LEV, TILE * half : TILE * half + TILE] = taken[
                        LEV * a : LEV * a + LEV, TILE * b : TILE * b + TILE
                    ]
        return jnp.dot(conv_l[f], dmat[...], preferred_element_type=F32)

    for p in (1, 2):
        feat[p] = convolve(0, p)

        @pl.loop(1, FIELDS)
        def _(f):
            feat[p] += convolve(f, p)

    for p in (0, 3):
        feat[p] = jnp.zeros((CHANNELS * LEV, COARSE), F32)

    for f in range(FIELDS):
        copy_x(0, f).wait_recv()
        copy_x(1, f).wait_recv()
        for side, first in enumerate((0, 24)):
            for row in range(4):
                st[f, first + row, :, :COLS] = recv_x[side, f, row].astype(F32)

        @pl.loop(0, 4)
        def _(i):
            first_step(f, 2 + i)
            first_step(f, 22 + i)

        @pl.loop(0, 4)
        def _(i):
            second_step(f, 2 + i)
            second_step(f, 18 + i)

        store(0, f).start()
        store(1, f).start()
        for p in (0, 3):
            feat[p] += convolve(f, p)

    for k in range(1, GY):
        pltpu.make_async_remote_copy(
            send_l.at[0],
            recv_l.at[lax.rem(gy + k, GY)],
            sl_sem.at[k],
            rl_sem.at[lax.rem(gy + k, GY)],
            device_id=(sec, gx, lax.rem(gy + k, GY)),
            device_id_type=MESH,
        ).wait_recv()
    base, depth = (
        jnp.concatenate(
            [
                (recv_l[4 * t, kind] + recv_l[4 * t + 1, kind])
                + (recv_l[4 * t + 2, kind] + recv_l[4 * t + 3, kind])
                for t in range(2)
            ],
            axis=1,
        )
        for kind in range(2)
    )
    level = sublanes((LEV, COARSE)).astype(F32)
    for p in range(4):
        score = [jnp.zeros((LEV, COARSE), F32) for _ in range(2)]
        for k in range(CHANNELS):
            value = jnp.maximum(feat[p, LEV * k : LEV * k + LEV, :] + conv_bias[k], 0.0)
            for c in range(2):
                score[c] = score[c] + readout[k, c] * value
        for c in range(2):
            prob = jax.nn.sigmoid(score[c] + readout_bias[c])
            at = 4 * c + p
            least, many = base[at : at + 1, :], depth[at : at + 1, :]
            inside = (level >= least) & (level < least + many)
            total = jnp.sum(jnp.where(inside, prob, 0.0), axis=0, keepdims=True)
            cf[at : at + 1, :] = total / many

    def copy_f(index, which, slot, where):
        return pltpu.make_async_remote_copy(
            cf,
            frac.at[which, slot],
            sf_sem.at[index],
            rf_sem.at[which, slot],
            device_id=where,
            device_id_type=MESH,
        )

    home = gy + 3
    away = jnp.where(near_high, gy - 5, jnp.minimum(gy + 11, SLOTS - 1))
    away_x = jnp.where(near_high, gx_high, gx_low)

    def each_send(act):
        for k in range(1, GY):
            act(copy_f(k, 0, home, (sec, gx, lax.rem(gy + k, GY))))
        for k, y in enumerate((0, GY - 1)):
            act(copy_f(8 + k, 1, home, (other, gx, y)))

        @pl.when(near_edge)
        def _():
            for k in range(GY):
                act(copy_f(10 + k, 0, away, (sec, away_x, k)))
            for k, y in enumerate((0, GY - 1)):
                act(copy_f(18 + k, 1, away, (other, away_x, y)))

    each_send(lambda copy: copy.start())
    frac[0, home] = cf[...]
    for slot in range(SLOTS):

        @pl.when(slot != home)
        def _():
            copy_f(0, 0, slot, (sec, gx, lax.rem(gy + 1, GY))).wait_recv()

    @pl.when(at_end)
    def _():
        for slot in range(SLOTS):
            copy_f(0, 1, slot, (sec, gx, lax.rem(gy + 1, GY))).wait_recv()

    shift = lax.rem(COARSE + HALF - 32 * gy, COARSE)
    rows = SLOTS * 8
    mine = pltpu.roll(frac[0].reshape(rows, COARSE), shift, 1)[:, :TILE]
    beyond = pltpu.roll(frac[1].reshape(rows, COARSE), shift, 1)[:, :TILE]
    place = lanes((rows, TILE))
    from_other = ((place < HALF) & (gy == 0)) | ((place >= HALF + 32) & (gy == GY - 1))
    window = jnp.where(from_other, beyond, mine)
    j, i = sublanes((TILE, 32)), lanes((TILE, 32))
    band_y = ((j >= i) & (j < i + WIN)).astype(F32)
    i, m = sublanes((64, rows)), lanes((64, rows))
    which, i = i // 32, lax.rem(i, 32)
    at_row = (m // 8) * 4 + lax.rem(m, 4)
    band_x = ((lax.rem(m, 8) // 4 == which) & (at_row >= i) & (at_row < i + WIN)).astype(F32)
    sums = jnp.dot(window, band_y, precision=lax.Precision.HIGHEST, preferred_element_type=F32)
    area = jnp.dot(band_x, sums, precision=lax.Precision.HIGHEST, preferred_element_type=F32)
    area = area * (1.0 / (WIN * WIN))
    own = pltpu.roll(window, TILE - HALF, 1)
    for c in range(2):
        area_out[c] = area[32 * c : 32 * c + 32, :]
        for k in range(GY):
            at = 8 * (k + 3) + 4 * c
            column_out[c, 4 * k : 4 * k + 4, :] = own[at : at + 4, 0:32]

    for side in range(2):
        for f in range(FIELDS):
            copy_x(side, f).wait_send()
    for k in range(3):
        copy_p(k).wait_send()
    for k in range(1, GY):
        copy_l(k).wait_send()
    each_send(lambda copy: copy.wait_send())
    for part in range(3):
        for f in range(FIELDS):
            store(part, f).wait()


def on_device(
    state, h_coeff, v_coeff, conv_weight, conv_bias, readout, readout_bias, level_base, level_depth
):
    vmem = pl.BlockSpec(memory_space=pltpu.VMEM)
    smem = pl.BlockSpec(memory_space=pltpu.SMEM)
    anywhere = pl.BlockSpec(memory_space=pl.ANY)
    dma = pltpu.SemaphoreType.DMA
    taps = KERNEL * KERNEL
    out, column_fraction, area_fraction = pl.pallas_call(
        kernel,
        out_shape=(
            jax.ShapeDtypeStruct((FIELDS, ROWS, LEV, COLS), F32),
            jax.ShapeDtypeStruct((2, 32, 32), F32),
            jax.ShapeDtypeStruct((2, 32, 32), F32),
        ),
        in_specs=[anywhere, vmem, vmem, vmem, smem, smem, smem, vmem, vmem],
        out_specs=(anywhere, vmem, vmem),
        scratch_shapes=[
            pltpu.VMEM((FIELDS, ROWS + 8, LEV, WIDE), F32),
            pltpu.VMEM((FIELDS, ROWS + 4, LEV, WIDE), F32),
            pltpu.VMEM((FIELDS, ROWS, LEV, COLS), F32),
            pltpu.VMEM((FIELDS, ROWS, LEV, COLS), BF16),
            pltpu.VMEM((FIELDS, 4, LEV, TILE), F32),
            pltpu.VMEM((2, FIELDS, 4, LEV, COLS), BF16),
            pltpu.VMEM((2, FIELDS, 4, LEV, COLS), BF16),
            pltpu.VMEM((5, LEV, TILE), F32),
            pltpu.VMEM((7, LEV, TILE), F32),
            pltpu.VMEM((GY, 2, 8, TILE), F32),
            pltpu.VMEM((GY, 2, 8, TILE), F32),
            pltpu.VMEM((KERNEL * TILE, KERNEL * TILE), BF16),
            pltpu.VMEM((FIELDS, CHANNELS * LEV, taps * LEV), BF16),
            pltpu.VMEM((taps * LEV, COARSE), BF16),
            pltpu.VMEM((4, CHANNELS * LEV, COARSE), F32),
            pltpu.VMEM((8, COARSE), F32),
            pltpu.VMEM((2, SLOTS, 8, COARSE), F32),
            dma((3, FIELDS)),
            dma((3, FIELDS)),
            dma((2, FIELDS)),
            dma((2, FIELDS)),
            dma((3,)),
            dma((3,)),
            dma((GY,)),
            dma((GY,)),
            dma((20,)),
            dma((2, SLOTS)),
        ],
        compiler_params=pltpu.CompilerParams(
            collective_id=0, has_side_effects=True, vmem_limit_bytes=56 * 2**20
        ),
        name="steps_and_fractions",
    )(
        jnp.transpose(state, (0, 2, 1, 3)),
        h_coeff,
        v_coeff,
        jnp.transpose(conv_weight, (1, 2, 0, 3)).reshape(taps * FIELDS, CHANNELS),
        conv_bias,
        readout,
        readout_bias,
        level_base,
        level_depth,
    )
    return jnp.transpose(out, (0, 2, 1, 3)), column_fraction, area_fraction


def solution(mesh):
    in_specs = (
        P(None, None, ("gx", "gy"), "sec"),
        P(),
        P(),
        P(),
        P(),
        P(),
        P(),
        P(None, "gx", ("sec", "gy")),
        P(None, "gx", ("sec", "gy")),
    )
    out_specs = (
        P(None, None, ("gx", "gy"), "sec"),
        P(None, "gx", ("sec", "gy")),
        P(None, "gx", ("sec", "gy")),
    )
    return jax.shard_map(
        on_device, mesh=mesh, in_specs=in_specs, out_specs=out_specs, check_vma=False
    )
```

```python
import jax
import jax.numpy as jnp
from jax import lax
from jax.experimental import pallas as pl
from jax.experimental.pallas import tpu as pltpu
from jax.sharding import PartitionSpec as P

F32 = jnp.float32
BF16 = jnp.bfloat16
MESH = pl.DeviceIdType.MESH

FIELDS = 4
LEV = 16
ROWS = 20
COLS = 1280
TILE = 128
TILES = COLS // TILE
WIDE = COLS + TILE
KERNEL = 5
CHANNELS = 32
COARSE = 256
WIN = 24
HALF = WIN // 2
GY = 8
GX = 8
SLOTS = 14


def lanes(shape):
    return lax.broadcasted_iota(jnp.int32, shape, len(shape) - 1)


def sublanes(shape):
    return lax.broadcasted_iota(jnp.int32, shape, len(shape) - 2)


def stencil(src, coef, band, f, rows, count, emit):
    lane = lanes((LEV, TILE))
    sub = sublanes((8, TILE))
    tiles = TILES + 1

    def at(r, t):
        return src[f, r, :, TILE * t : TILE * t + TILE]

    parts = []
    for r in rows:
        for t in range(tiles):
            value = at(r, t)
            head = value.astype(BF16)
            tail = (value - head.astype(F32)).astype(BF16)
            parts.append(jnp.concatenate([head, tail], axis=1))
    sums = jnp.dot(jnp.concatenate(parts, axis=0), band[...], preferred_element_type=F32)

    c0, c1, c2 = coef[f, 0], coef[f, 1], coef[f, 2]
    for q, r in enumerate(rows):

        def along_y(t, part):
            first = LEV * (q * tiles + t % tiles)
            return sums[first : first + LEV, TILE * part : TILE * part + TILE]

        for t in range(count):
            value = at(r, t)
            y = along_y(t, 0) + jnp.where(lane < 64, along_y(t - 1, 1), along_y(t + 1, 1))
            low, high = value[:8], value[8:]
            low_down, high_down = pltpu.roll(low, 1, 0), pltpu.roll(high, 1, 0)
            low_up, high_up = pltpu.roll(low, 7, 0), pltpu.roll(high, 7, 0)
            vert = jnp.concatenate(
                [
                    jnp.where(sub == 0, 0.0, low_down) + jnp.where(sub == 7, high_up, low_up),
                    jnp.where(sub == 0, low_down, high_down) + jnp.where(sub == 7, 0.0, high_up),
                ],
                axis=0,
            )
            x = 16.0 * (at(r - 1, t) + at(r + 1, t)) - (at(r - 2, t) + at(r + 2, t))
            emit(r, t, (c0 * value + c1 * (x + y)) + c2 * vert)


def kernel(
    state,
    h_coeff,
    v_coeff,
    weight,
    conv_bias,
    readout,
    readout_bias,
    level_base,
    level_depth,
    adv,
    column_out,
    area_out,
    st,
    u,
    ab,
    coef,
    band,
    send_x,
    recv_x,
    send_p,
    recv_p,
    send_l,
    recv_l,
    select,
    taps_w,
    conv_l,
    dmat,
    feat,
    cf,
    frac,
    load_sem,
    sx_sem,
    rx_sem,
    sp_sem,
    rp_sem,
    sl_sem,
    rl_sem,
    sf_sem,
    rf_sem,
):
    sec, gx, gy = lax.axis_index("sec"), lax.axis_index("gx"), lax.axis_index("gy")
    other = 1 - sec
    gx_low, gx_high = lax.rem(gx + GX - 1, GX), lax.rem(gx + 1, GX)
    brick = gx * GY + gy
    low, high = lax.rem(brick + GX * GY - 1, GX * GY), lax.rem(brick + 1, GX * GY)
    low_x, low_y, high_x, high_y = low // GY, lax.rem(low, GY), high // GY, lax.rem(high, GY)
    near_low, near_high = gy <= 2, gy >= 5
    near_edge = near_low | near_high
    at_end = (gy == 0) | (gy == GY - 1)

    spans = ((0, 4), (16, 4), (4, 12))
    loads = []
    for part, (first, count) in enumerate(spans):
        for f in range(FIELDS):
            copy = pltpu.make_async_copy(
                state.at[f, pl.ds(first, count)],
                st.at[f, pl.ds(first + 4, count), :, pl.ds(0, COLS)],
                load_sem.at[part, f],
            )
            copy.start()
            loads.append(copy)

    barrier = pltpu.get_barrier_semaphore()

    def hello(where):
        pl.semaphore_signal(barrier, inc=1, device_id=where, device_id_type=MESH)

    hello((sec, low_x, low_y))
    hello((sec, high_x, high_y))
    hello((other, gx, gy))
    hello((other, low_x, low_y))
    hello((other, high_x, high_y))
    for k in range(1, GY):
        hello((sec, gx, lax.rem(gy + k, GY)))
    for k in range(3):
        hello((sec, gx_high, k))
        hello((sec, gx_low, 5 + k))

    @pl.when(at_end)
    def _():
        for k in range(GY):
            hello((other, gx, k))
        for k in range(3):
            hello((other, gx_high, k))
            hello((other, gx_low, 5 + k))

    eye = (sublanes((LEV, LEV)) == lanes((LEV, LEV))).astype(F32)
    for f in range(FIELDS):
        horiz = jnp.sum(eye * h_coeff[f : f + 1, :], axis=1, keepdims=True)
        vertical = jnp.sum(eye * v_coeff[f : f + 1, :], axis=1, keepdims=True)
        for k, value in enumerate(
            (
                1.0 - 5.0 * horiz - 2.0 * vertical,
                horiz * (1.0 / 12.0),
                vertical,
            )
        ):
            coef[f, k] = jnp.broadcast_to(value, (LEV, TILE))

    i, j = sublanes((2 * TILE, 2 * TILE)), lanes((2 * TILE, 2 * TILE))
    away = jnp.abs(lax.rem(i, TILE) - lax.rem(j, TILE))
    away = jnp.where(j < TILE, away, TILE - away)
    taps_y = jnp.where(away == 1, 16.0, jnp.where(away == 2, -1.0, 0.0))
    band[...] = taps_y.astype(BF16)

    for copy in loads[: 2 * FIELDS]:
        copy.wait()

    lane = lanes((LEV, TILE))
    group_of = lax.rem(lane + 4, TILE) // 8

    @pl.loop(0, FIELDS)
    def _(f):
        for side, first in enumerate((4, 20)):
            for row in range(4):
                send_x[side, f, row] = st[f, first + row, :, :COLS].astype(BF16)

    def edge(f, row):
        return jnp.where(lane < 64, st[f, row, :, :TILE], st[f, row, :, COLS - TILE : COLS])

    def pack(group):
        total = jnp.zeros((LEV, TILE), F32)
        for j in range(16):
            part = pltpu.roll(edge(j // 4, 4 + 4 * group + j % 4), 8 * j, 1)
            total = jnp.where(group_of == j, part, total)
        send_p[group] = total

    pack(0)
    pack(4)

    for copy in loads[2 * FIELDS :]:
        copy.wait()
    for group in range(1, 4):
        pack(group)

    pl.semaphore_wait(barrier, 14 + jnp.where(near_edge, 10, 0))

    def copy_x(side, f):
        where = (sec, low_x, low_y) if side == 0 else (sec, high_x, high_y)
        return pltpu.make_async_remote_copy(
            send_x.at[side, f],
            recv_x.at[1 - side, f],
            sx_sem.at[side, f],
            rx_sem.at[1 - side, f],
            device_id=where,
            device_id_type=MESH,
        )

    def copy_p(k):
        source, target, where = (
            (send_p, recv_p.at[pl.ds(1, 5)], (other, gx, gy)),
            (send_p.at[0:1], recv_p.at[pl.ds(6, 1)], (other, low_x, low_y)),
            (send_p.at[4:5], recv_p.at[pl.ds(0, 1)], (other, high_x, high_y)),
        )[k]
        return pltpu.make_async_remote_copy(
            source, target, sp_sem.at[k], rp_sem.at[k], device_id=where, device_id_type=MESH
        )

    def copy_l(k):
        to = lax.rem(gy + k, GY)
        return pltpu.make_async_remote_copy(
            send_l.at[to],
            recv_l.at[gy],
            sl_sem.at[k],
            rl_sem.at[gy],
            device_id=(sec, gx, to),
            device_id_type=MESH,
        )

    for k in range(3):
        copy_p(k).start()
    for f in range(FIELDS):
        copy_x(0, f).start()
        copy_x(1, f).start()

    send_l[...] = jnp.zeros_like(send_l)
    for k in range(GY):
        for c in range(2):
            for kind, ref in enumerate((level_base, level_depth)):
                send_l[k, kind, 4 * c : 4 * c + 4, 0:32] = ref[c, 4 * k : 4 * k + 4, :].astype(F32)
    turn = 32 * lax.rem(gy, 4)
    for k in range(GY):
        for kind in range(2):
            send_l[k, kind] = pltpu.roll(send_l[k, kind], turn, 1)
    for k in range(1, GY):
        copy_l(k).start()
    recv_l[gy] = send_l[gy]

    row = sublanes((KERNEL * TILE, TILE))
    col = lanes((KERNEL * TILE, TILE))
    for b in range(KERNEL):
        select[:, TILE * b : TILE * b + TILE] = (row == KERNEL * col + b).astype(F32).astype(BF16)
    taps = KERNEL * KERNEL
    for tap in range(taps):
        taps_w[FIELDS * tap : FIELDS * tap + FIELDS, :] = weight[tap // KERNEL, tap % KERNEL].astype(F32)
    shape = (CHANNELS * LEV, CHANNELS)
    spread = (sublanes(shape) // LEV == lanes(shape)).astype(F32).astype(BF16)
    wide_w = lax.dot_general(
        spread,
        taps_w[...].astype(BF16),
        (((1,), (1,)), ((), ())),
        preferred_element_type=F32,
    ).astype(BF16)
    shape = (taps * FIELDS, FIELDS * taps * LEV)
    tap_at = lanes(shape) // LEV
    pick = (sublanes(shape) == lax.rem(tap_at, taps) * FIELDS + tap_at // taps).astype(F32)
    full = jnp.dot(wide_w, pick.astype(BF16), preferred_element_type=F32)
    same = lax.rem(sublanes(full.shape), LEV) == lax.rem(lanes(full.shape), LEV)
    conv_l[...] = jnp.where(same, full, 0.0).astype(BF16)

    def unpack(group):
        for j in range(16):
            st[j // 4, 4 * group + j % 4, :, COLS:] = pltpu.roll(
                recv_p[group], (TILE - 8 * j) % TILE, 1
            )

    copy_p(0).wait_recv()
    for group in range(1, 6):
        unpack(group)

    def first_step(f, rows):
        def emit(r, t, value):
            u[f, r - 2, :, TILE * t : TILE * t + TILE] = value

        stencil(st, coef, band, f, rows, TILES + 1, emit)

    def second_step(f, rows):
        def emit(r, t, value):
            adv[f, r - 2, :, TILE * t : TILE * t + TILE] = value
            ab[f, r - 2, :, TILE * t : TILE * t + TILE] = value.astype(BF16)

        stencil(u, coef, band, f, rows, TILES, emit)

    @pl.loop(0, FIELDS)
    def _(f):
        first_step(f, range(6, 14))
        first_step(f, range(14, 22))
        second_step(f, range(6, 18))

    def take(f, pair, slot):
        blocks = [
            ab[f, KERNEL * p : KERNEL * p + KERNEL, :, 640 * half : 640 * half + 640].reshape(
                KERNEL * LEV, KERNEL * TILE
            )
            for p in pair
            for half in range(2)
        ]
        taken = jnp.dot(
            jnp.concatenate(blocks, axis=0), select[...], preferred_element_type=F32
        ).astype(BF16)
        for i in range(2):
            for half in range(2):
                for a in range(KERNEL):
                    first = LEV * (KERNEL * (2 * i + half) + a)
                    for b in range(KERNEL):
                        tap = LEV * (taps * f + KERNEL * a + b)
                        dmat[slot, i, tap : tap + LEV, TILE * half : TILE * half + TILE] = taken[
                            first : first + LEV, TILE * b : TILE * b + TILE
                        ]

    for f in range(FIELDS):
        take(f, (1, 2), 0)
    for i, p in enumerate((1, 2)):
        feat[p] = jnp.dot(conv_l[...], dmat[0, i], preferred_element_type=F32)

    for k in range(1, 3):
        copy_p(k).wait_recv()
    unpack(0)
    unpack(6)
    early = 9 * TILE
    for f in range(FIELDS):
        copy_x(0, f).wait_recv()
        copy_x(1, f).wait_recv()
        for side, first in enumerate((0, 24)):
            for row in range(4):
                st[f, first + row, :, :COLS] = recv_x[side, f, row].astype(F32)

        first_step(f, (2, 3, 4, 5, 22, 23, 24, 25))
        second_step(f, (2, 3, 4, 5, 18, 19, 20, 21))
        take(f, (0, 3), 1)
        if f == 2:
            for i, p in enumerate((0, 3)):
                feat[p] = jnp.dot(
                    conv_l[:, :early], dmat[1, i, :early], preferred_element_type=F32
                )
    for i, p in enumerate((0, 3)):
        feat[p] += jnp.dot(conv_l[:, early:], dmat[1, i, early:], preferred_element_type=F32)

    for k in range(1, GY):
        pltpu.make_async_remote_copy(
            send_l.at[0],
            recv_l.at[lax.rem(gy + k, GY)],
            sl_sem.at[k],
            rl_sem.at[lax.rem(gy + k, GY)],
            device_id=(sec, gx, lax.rem(gy + k, GY)),
            device_id_type=MESH,
        ).wait_recv()
    base, depth = (
        jnp.concatenate(
            [
                (recv_l[4 * t, kind] + recv_l[4 * t + 1, kind])
                + (recv_l[4 * t + 2, kind] + recv_l[4 * t + 3, kind])
                for t in range(2)
            ],
            axis=1,
        )
        for kind in range(2)
    )
    level = sublanes((LEV, COARSE)).astype(F32)
    for p in range(4):
        score = [jnp.zeros((LEV, COARSE), F32) for _ in range(2)]
        for k in range(CHANNELS):
            value = jnp.maximum(feat[p, LEV * k : LEV * k + LEV, :] + conv_bias[k], 0.0)
            for c in range(2):
                score[c] = score[c] + readout[c, k] * value
        for c in range(2):
            prob = jax.nn.sigmoid(score[c] + readout_bias[c])
            at = 4 * c + p
            least, many = base[at : at + 1, :], depth[at : at + 1, :]
            inside = (level >= least) & (level < least + many)
            total = jnp.sum(jnp.where(inside, prob, 0.0), axis=0, keepdims=True)
            cf[at : at + 1, :] = total / many

    def copy_f(index, which, slot, where):
        return pltpu.make_async_remote_copy(
            cf,
            frac.at[which, slot],
            sf_sem.at[index],
            rf_sem.at[which, slot],
            device_id=where,
            device_id_type=MESH,
        )

    home = gy + 3
    away = jnp.where(near_high, gy - 5, jnp.minimum(gy + 11, SLOTS - 1))
    away_x = jnp.where(near_high, gx_high, gx_low)

    def each_send(act):
        for k in range(1, GY):
            act(copy_f(k, 0, home, (sec, gx, lax.rem(gy + k, GY))))
        for k, y in enumerate((0, GY - 1)):
            act(copy_f(8 + k, 1, home, (other, gx, y)))

        @pl.when(near_edge)
        def _():
            for k in range(GY):
                act(copy_f(10 + k, 0, away, (sec, away_x, k)))
            for k, y in enumerate((0, GY - 1)):
                act(copy_f(18 + k, 1, away, (other, away_x, y)))

    each_send(lambda copy: copy.start())
    frac[0, home] = cf[...]
    for slot in range(SLOTS):

        @pl.when(slot != home)
        def _():
            copy_f(0, 0, slot, (sec, gx, lax.rem(gy + 1, GY))).wait_recv()

    @pl.when(at_end)
    def _():
        for slot in range(SLOTS):
            copy_f(0, 1, slot, (sec, gx, lax.rem(gy + 1, GY))).wait_recv()

    shift = lax.rem(COARSE + HALF - 32 * gy, COARSE)
    rows = SLOTS * 8
    mine = pltpu.roll(frac[0].reshape(rows, COARSE), shift, 1)[:, :TILE]
    beyond = pltpu.roll(frac[1].reshape(rows, COARSE), shift, 1)[:, :TILE]
    place = lanes((rows, TILE))
    from_other = ((place < HALF) & (gy == 0)) | ((place >= HALF + 32) & (gy == GY - 1))
    window = jnp.where(from_other, beyond, mine)
    j, i = sublanes((TILE, 32)), lanes((TILE, 32))
    band_y = ((j >= i) & (j < i + WIN)).astype(F32)
    i, m = sublanes((64, rows)), lanes((64, rows))
    which, i = i // 32, lax.rem(i, 32)
    at_row = (m // 8) * 4 + lax.rem(m, 4)
    band_x = ((lax.rem(m, 8) // 4 == which) & (at_row >= i) & (at_row < i + WIN)).astype(F32)
    sums = jnp.dot(window, band_y, precision=lax.Precision.HIGHEST, preferred_element_type=F32)
    area = jnp.dot(band_x, sums, precision=lax.Precision.HIGHEST, preferred_element_type=F32)
    area = area * (1.0 / (WIN * WIN))
    own = pltpu.roll(window, TILE - HALF, 1)
    for c in range(2):
        area_out[c] = area[32 * c : 32 * c + 32, :]
        for k in range(GY):
            at = 8 * (k + 3) + 4 * c
            column_out[c, 4 * k : 4 * k + 4, :] = own[at : at + 4, 0:32]

    for side in range(2):
        for f in range(FIELDS):
            copy_x(side, f).wait_send()
    for k in range(3):
        copy_p(k).wait_send()
    for k in range(1, GY):
        copy_l(k).wait_send()
    each_send(lambda copy: copy.wait_send())


def write_out(adv, column_fraction, area_fraction, out, column_out, area_out, sem):
    copies = [
        pltpu.make_async_copy(adv.at[f], out.at[f], sem.at[f]) for f in range(FIELDS)
    ] + [
        pltpu.make_async_copy(column_fraction, column_out, sem.at[FIELDS]),
        pltpu.make_async_copy(area_fraction, area_out, sem.at[FIELDS + 1]),
    ]
    for copy in copies:
        copy.start()
    for copy in copies:
        copy.wait()


def on_device(
    state, h_coeff, v_coeff, conv_weight, conv_bias, readout, readout_bias, level_base, level_depth
):
    vmem = pl.BlockSpec(memory_space=pltpu.VMEM)
    smem = pl.BlockSpec(memory_space=pltpu.SMEM)
    anywhere = pl.BlockSpec(memory_space=pl.ANY)
    dma = pltpu.SemaphoreType.DMA
    taps = KERNEL * KERNEL
    out, column_fraction, area_fraction = pl.pallas_call(
        kernel,
        out_shape=(
            pltpu.VMEM((FIELDS, ROWS, LEV, COLS), F32),
            pltpu.VMEM((2, 32, 32), F32),
            pltpu.VMEM((2, 32, 32), F32),
        ),
        in_specs=[anywhere, vmem, vmem, vmem, smem, smem, smem, vmem, vmem],
        out_specs=(vmem, vmem, vmem),
        scratch_shapes=[
            pltpu.VMEM((FIELDS, ROWS + 8, LEV, WIDE), F32),
            pltpu.VMEM((FIELDS, ROWS + 4, LEV, WIDE), F32),
            pltpu.VMEM((FIELDS, ROWS, LEV, COLS), BF16),
            pltpu.VMEM((FIELDS, 3, LEV, TILE), F32),
            pltpu.VMEM((2 * TILE, 2 * TILE), BF16),
            pltpu.VMEM((2, FIELDS, 4, LEV, COLS), BF16),
            pltpu.VMEM((2, FIELDS, 4, LEV, COLS), BF16),
            pltpu.VMEM((5, LEV, TILE), F32),
            pltpu.VMEM((7, LEV, TILE), F32),
            pltpu.VMEM((GY, 2, 8, TILE), F32),
            pltpu.VMEM((GY, 2, 8, TILE), F32),
            pltpu.VMEM((KERNEL * TILE, KERNEL * TILE), BF16),
            pltpu.VMEM((taps * FIELDS, CHANNELS), F32),
            pltpu.VMEM((CHANNELS * LEV, FIELDS * taps * LEV), BF16),
            pltpu.VMEM((2, 2, FIELDS * taps * LEV, COARSE), BF16),
            pltpu.VMEM((4, CHANNELS * LEV, COARSE), F32),
            pltpu.VMEM((8, COARSE), F32),
            pltpu.VMEM((2, SLOTS, 8, COARSE), F32),
            dma((3, FIELDS)),
            dma((2, FIELDS)),
            dma((2, FIELDS)),
            dma((3,)),
            dma((3,)),
            dma((GY,)),
            dma((GY,)),
            dma((20,)),
            dma((2, SLOTS)),
        ],
        compiler_params=pltpu.CompilerParams(
            collective_id=0, has_side_effects=True, vmem_limit_bytes=48 * 2**20
        ),
        name="steps_and_fractions",
    )(
        jnp.transpose(state, (0, 2, 1, 3)),
        h_coeff,
        v_coeff,
        jnp.transpose(conv_weight, (1, 2, 0, 3)),
        conv_bias,
        jnp.transpose(readout),
        readout_bias,
        level_base,
        level_depth,
    )
    out, column_fraction, area_fraction = pl.pallas_call(
        write_out,
        out_shape=(
            jax.ShapeDtypeStruct((FIELDS, ROWS, LEV, COLS), F32),
            jax.ShapeDtypeStruct((2, 32, 32), F32),
            jax.ShapeDtypeStruct((2, 32, 32), F32),
        ),
        in_specs=[vmem, vmem, vmem],
        out_specs=(anywhere, anywhere, anywhere),
        scratch_shapes=[dma((FIELDS + 2,))],
        compiler_params=pltpu.CompilerParams(vmem_limit_bytes=2**20),
        name="write_out",
    )(out, column_fraction, area_fraction)
    return jnp.transpose(out, (0, 2, 1, 3)), column_fraction, area_fraction


def solution(mesh):
    in_specs = (
        P(None, None, ("gx", "gy"), "sec"),
        P(),
        P(),
        P(),
        P(),
        P(),
        P(),
        P(None, "gx", ("sec", "gy")),
        P(None, "gx", ("sec", "gy")),
    )
    out_specs = (
        P(None, None, ("gx", "gy"), "sec"),
        P(None, "gx", ("sec", "gy")),
        P(None, "gx", ("sec", "gy")),
    )
    return jax.shard_map(
        on_device, mesh=mesh, in_specs=in_specs, out_specs=out_specs, check_vma=False
    )
```

```python
import jax
import jax.numpy as jnp
from jax import lax
from jax.experimental import pallas as pl
from jax.experimental.pallas import tpu as pltpu
from jax.sharding import PartitionSpec as P

F32 = jnp.float32
BF16 = jnp.bfloat16
MESH = pl.DeviceIdType.MESH

FIELDS = 4
LEV = 16
ROWS = 20
COLS = 1280
TILE = 128
TILES = COLS // TILE
WIDE = COLS + TILE
KERNEL = 5
CHANNELS = 32
COARSE = 256
WIN = 24
HALF = WIN // 2
GY = 8
GX = 8
SLOTS = 14


def lanes(shape):
    return lax.broadcasted_iota(jnp.int32, shape, len(shape) - 1)


def sublanes(shape):
    return lax.broadcasted_iota(jnp.int32, shape, len(shape) - 2)


def stencil(src, coef, band, f, rows, wanted, emit):
    lane = lanes((LEV, TILE))
    sub = sublanes((8, TILE))
    tiles = TILES + 1
    needed = sorted({(t + d) % tiles for t in wanted for d in (-1, 0, 1)})

    def at(r, t):
        return src[f, r, :, TILE * t : TILE * t + TILE]

    parts = []
    for r in rows:
        for t in needed:
            value = at(r, t)
            head = value.astype(BF16)
            tail = (value - head.astype(F32)).astype(BF16)
            parts.append(jnp.concatenate([head, tail], axis=1))
    sums = jnp.dot(jnp.concatenate(parts, axis=0), band[...], preferred_element_type=F32)

    c0, c1, c2 = coef[f, 0], coef[f, 1], coef[f, 2]
    for q, r in enumerate(rows):

        def along_y(t, part):
            first = LEV * (q * len(needed) + needed.index(t % tiles))
            return sums[first : first + LEV, TILE * part : TILE * part + TILE]

        for t in wanted:
            value = at(r, t)
            y = along_y(t, 0) + jnp.where(lane < 64, along_y(t - 1, 1), along_y(t + 1, 1))
            low, high = value[:8], value[8:]
            low_down, high_down = pltpu.roll(low, 1, 0), pltpu.roll(high, 1, 0)
            low_up, high_up = pltpu.roll(low, 7, 0), pltpu.roll(high, 7, 0)
            vert = jnp.concatenate(
                [
                    jnp.where(sub == 0, 0.0, low_down) + jnp.where(sub == 7, high_up, low_up),
                    jnp.where(sub == 0, low_down, high_down) + jnp.where(sub == 7, 0.0, high_up),
                ],
                axis=0,
            )
            x = 16.0 * (at(r - 1, t) + at(r + 1, t)) - (at(r - 2, t) + at(r + 2, t))
            emit(r, t, (c0 * value + c1 * (x + y)) + c2 * vert)


def kernel(
    state,
    h_coeff,
    v_coeff,
    weight,
    conv_bias,
    readout,
    readout_bias,
    level_base,
    level_depth,
    adv,
    column_out,
    area_out,
    st,
    u,
    ab,
    coef,
    band,
    send_x,
    recv_x,
    send_p,
    recv_p,
    send_l,
    recv_l,
    select,
    taps_w,
    conv_l,
    dmat,
    feat,
    cf,
    frac,
    load_sem,
    sx_sem,
    rx_sem,
    sp_sem,
    rp_sem,
    sl_sem,
    rl_sem,
    sf_sem,
    rf_sem,
):
    sec, gx, gy = lax.axis_index("sec"), lax.axis_index("gx"), lax.axis_index("gy")
    other = 1 - sec
    gx_low, gx_high = lax.rem(gx + GX - 1, GX), lax.rem(gx + 1, GX)
    brick = gx * GY + gy
    low, high = lax.rem(brick + GX * GY - 1, GX * GY), lax.rem(brick + 1, GX * GY)
    low_x, low_y, high_x, high_y = low // GY, lax.rem(low, GY), high // GY, lax.rem(high, GY)
    near_low, near_high = gy <= 2, gy >= 5
    near_edge = near_low | near_high
    at_end = (gy == 0) | (gy == GY - 1)

    spans = ((0, 4), (16, 4), (4, 12))
    loads = []
    for part, (first, count) in enumerate(spans):
        for f in range(FIELDS):
            copy = pltpu.make_async_copy(
                state.at[f, pl.ds(first, count)],
                st.at[f, pl.ds(first + 4, count), :, pl.ds(0, COLS)],
                load_sem.at[part, f],
            )
            copy.start()
            loads.append(copy)

    barrier = pltpu.get_barrier_semaphore()

    def hello(where):
        pl.semaphore_signal(barrier, inc=1, device_id=where, device_id_type=MESH)

    hello((sec, low_x, low_y))
    hello((sec, high_x, high_y))
    hello((other, gx, gy))
    hello((other, low_x, low_y))
    hello((other, high_x, high_y))
    for k in range(1, GY):
        hello((sec, gx, lax.rem(gy + k, GY)))
    for k in range(3):
        hello((sec, gx_high, k))
        hello((sec, gx_low, 5 + k))

    @pl.when(at_end)
    def _():
        for k in range(GY):
            hello((other, gx, k))
        for k in range(3):
            hello((other, gx_high, k))
            hello((other, gx_low, 5 + k))

    for copy in loads[: 2 * FIELDS]:
        copy.wait()

    lane = lanes((LEV, TILE))
    group_of = lax.rem(lane + 4, TILE) // 8

    @pl.loop(0, FIELDS)
    def _(f):
        for side, first in enumerate((4, 20)):
            for row in range(4):
                send_x[side, f, row] = st[f, first + row, :, :COLS].astype(BF16)

    pl.semaphore_wait(barrier, 14 + jnp.where(near_edge, 10, 0))

    def copy_x(side, f):
        where = (sec, low_x, low_y) if side == 0 else (sec, high_x, high_y)
        return pltpu.make_async_remote_copy(
            send_x.at[side, f],
            recv_x.at[1 - side, f],
            sx_sem.at[side, f],
            rx_sem.at[1 - side, f],
            device_id=where,
            device_id_type=MESH,
        )

    def copy_p(k):
        source, target, where = (
            (send_p, recv_p.at[pl.ds(1, 5)], (other, gx, gy)),
            (send_p.at[0:1], recv_p.at[pl.ds(6, 1)], (other, low_x, low_y)),
            (send_p.at[4:5], recv_p.at[pl.ds(0, 1)], (other, high_x, high_y)),
        )[k]
        return pltpu.make_async_remote_copy(
            source, target, sp_sem.at[k], rp_sem.at[k], device_id=where, device_id_type=MESH
        )

    def copy_l(k):
        to = lax.rem(gy + k, GY)
        return pltpu.make_async_remote_copy(
            send_l.at[to],
            recv_l.at[gy],
            sl_sem.at[k],
            rl_sem.at[gy],
            device_id=(sec, gx, to),
            device_id_type=MESH,
        )

    for f in range(FIELDS):
        copy_x(0, f).start()
        copy_x(1, f).start()

    def edge(f, row):
        return jnp.where(lane < 64, st[f, row, :, :TILE], st[f, row, :, COLS - TILE : COLS])

    def pack(group):
        total = jnp.zeros((LEV, TILE), F32)
        for j in range(16):
            part = pltpu.roll(edge(j // 4, 4 + 4 * group + j % 4), 8 * j, 1)
            total = jnp.where(group_of == j, part, total)
        send_p[group] = total

    for copy in loads[2 * FIELDS :]:
        copy.wait()
    for group in range(5):
        pack(group)

    for k in range(3):
        copy_p(k).start()

    eye = (sublanes((LEV, LEV)) == lanes((LEV, LEV))).astype(F32)
    for f in range(FIELDS):
        horiz = jnp.sum(eye * h_coeff[f : f + 1, :], axis=1, keepdims=True)
        vertical = jnp.sum(eye * v_coeff[f : f + 1, :], axis=1, keepdims=True)
        for k, value in enumerate(
            (
                1.0 - 5.0 * horiz - 2.0 * vertical,
                horiz * (1.0 / 12.0),
                vertical,
            )
        ):
            coef[f, k] = jnp.broadcast_to(value, (LEV, TILE))

    i, j = sublanes((2 * TILE, 2 * TILE)), lanes((2 * TILE, 2 * TILE))
    away = jnp.abs(lax.rem(i, TILE) - lax.rem(j, TILE))
    away = jnp.where(j < TILE, away, TILE - away)
    taps_y = jnp.where(away == 1, 16.0, jnp.where(away == 2, -1.0, 0.0))
    band[...] = taps_y.astype(BF16)


    send_l[...] = jnp.zeros_like(send_l)
    for k in range(GY):
        for c in range(2):
            for kind, ref in enumerate((level_base, level_depth)):
                send_l[k, kind, 4 * c : 4 * c + 4, 0:32] = ref[c, 4 * k : 4 * k + 4, :].astype(F32)
    turn = 32 * lax.rem(gy, 4)
    for k in range(GY):
        for kind in range(2):
            send_l[k, kind] = pltpu.roll(send_l[k, kind], turn, 1)
    for k in range(1, GY):
        copy_l(k).start()
    recv_l[gy] = send_l[gy]

    row = sublanes((KERNEL * TILE, TILE))
    col = lanes((KERNEL * TILE, TILE))
    for b in range(KERNEL):
        select[:, TILE * b : TILE * b + TILE] = (row == KERNEL * col + b).astype(F32).astype(BF16)
    taps = KERNEL * KERNEL
    for tap in range(taps):
        taps_w[FIELDS * tap : FIELDS * tap + FIELDS, :] = weight[tap // KERNEL, tap % KERNEL].astype(F32)
    shape = (CHANNELS * LEV, CHANNELS)
    spread = (sublanes(shape) // LEV == lanes(shape)).astype(F32).astype(BF16)
    wide_w = lax.dot_general(
        spread,
        taps_w[...].astype(BF16),
        (((1,), (1,)), ((), ())),
        preferred_element_type=F32,
    ).astype(BF16)
    shape = (taps * FIELDS, FIELDS * taps * LEV)
    tap_at = lanes(shape) // LEV
    pick = (sublanes(shape) == lax.rem(tap_at, taps) * FIELDS + tap_at // taps).astype(F32)
    full = jnp.dot(wide_w, pick.astype(BF16), preferred_element_type=F32)
    same = lax.rem(sublanes(full.shape), LEV) == lax.rem(lanes(full.shape), LEV)
    conv_l[...] = jnp.where(same, full, 0.0).astype(BF16)

    def unpack(group):
        for j in range(16):
            st[j // 4, 4 * group + j % 4, :, COLS:] = pltpu.roll(
                recv_p[group], (TILE - 8 * j) % TILE, 1
            )

    @pl.loop(0, FIELDS)
    def _(f):
        for r in range(4, ROWS + 4):
            st[f, r, :, COLS:] = jnp.zeros((LEV, TILE), F32)

    def first_step(f, rows, wanted=range(TILES + 1)):
        def emit(r, t, value):
            u[f, r - 2, :, TILE * t : TILE * t + TILE] = value

        stencil(st, coef, band, f, rows, wanted, emit)

    def second_step(f, rows, wanted=range(TILES)):
        def emit(r, t, value):
            adv[f, r - 2, :, TILE * t : TILE * t + TILE] = value
            ab[f, r - 2, :, TILE * t : TILE * t + TILE] = value.astype(BF16)

        stencil(u, coef, band, f, rows, wanted, emit)

    @pl.loop(0, FIELDS)
    def _(f):
        first_step(f, range(6, 14))
        first_step(f, range(14, 22))
        second_step(f, range(6, 18))

    def take(f, pair, slot):
        blocks = [
            ab[f, KERNEL * p : KERNEL * p + KERNEL, :, 640 * half : 640 * half + 640].reshape(
                KERNEL * LEV, KERNEL * TILE
            )
            for p in pair
            for half in range(2)
        ]
        taken = jnp.dot(
            jnp.concatenate(blocks, axis=0), select[...], preferred_element_type=F32
        ).astype(BF16)
        for i in range(2):
            for half in range(2):
                for a in range(KERNEL):
                    first = LEV * (KERNEL * (2 * i + half) + a)
                    for b in range(KERNEL):
                        tap = LEV * (taps * f + KERNEL * a + b)
                        dmat[slot, i, tap : tap + LEV, TILE * half : TILE * half + TILE] = taken[
                            first : first + LEV, TILE * b : TILE * b + TILE
                        ]

    copy_p(0).wait_recv()
    for group in range(1, 6):
        unpack(group)

    @pl.loop(0, FIELDS)
    def _(f):
        first_step(f, range(6, 22), (TILES - 1, TILES, 0))
        second_step(f, range(6, 18), (TILES - 1, 0))

    for f in range(FIELDS):
        take(f, (1, 2), 0)
    for i, p in enumerate((1, 2)):
        feat[p] = jnp.dot(conv_l[...], dmat[0, i], preferred_element_type=F32)

    for k in range(1, 3):
        copy_p(k).wait_recv()
    unpack(0)
    unpack(6)
    early = 9 * TILE
    for f in range(FIELDS):
        copy_x(0, f).wait_recv()
        copy_x(1, f).wait_recv()
        for side, first in enumerate((0, 24)):
            for row in range(4):
                st[f, first + row, :, :COLS] = recv_x[side, f, row].astype(F32)

        first_step(f, (2, 3, 4, 5, 22, 23, 24, 25))
        second_step(f, (2, 3, 4, 5, 18, 19, 20, 21))
        take(f, (0, 3), 1)
        if f == 2:
            for i, p in enumerate((0, 3)):
                feat[p] = jnp.dot(
                    conv_l[:, :early], dmat[1, i, :early], preferred_element_type=F32
                )
    for i, p in enumerate((0, 3)):
        feat[p] += jnp.dot(conv_l[:, early:], dmat[1, i, early:], preferred_element_type=F32)

    for k in range(1, GY):
        pltpu.make_async_remote_copy(
            send_l.at[0],
            recv_l.at[lax.rem(gy + k, GY)],
            sl_sem.at[k],
            rl_sem.at[lax.rem(gy + k, GY)],
            device_id=(sec, gx, lax.rem(gy + k, GY)),
            device_id_type=MESH,
        ).wait_recv()
    base, depth = (
        jnp.concatenate(
            [
                (recv_l[4 * t, kind] + recv_l[4 * t + 1, kind])
                + (recv_l[4 * t + 2, kind] + recv_l[4 * t + 3, kind])
                for t in range(2)
            ],
            axis=1,
        )
        for kind in range(2)
    )
    level = sublanes((LEV, COARSE)).astype(F32)
    for p in range(4):
        score = [jnp.zeros((LEV, COARSE), F32) for _ in range(2)]
        for k in range(CHANNELS):
            value = jnp.maximum(feat[p, LEV * k : LEV * k + LEV, :] + conv_bias[k], 0.0)
            for c in range(2):
                score[c] = score[c] + readout[c, k] * value
        for c in range(2):
            prob = jax.nn.sigmoid(score[c] + readout_bias[c])
            at = 4 * c + p
            least, many = base[at : at + 1, :], depth[at : at + 1, :]
            inside = (level >= least) & (level < least + many)
            total = jnp.sum(jnp.where(inside, prob, 0.0), axis=0, keepdims=True)
            cf[at : at + 1, :] = total / many

    def copy_f(index, which, slot, where):
        return pltpu.make_async_remote_copy(
            cf,
            frac.at[which, slot],
            sf_sem.at[index],
            rf_sem.at[which, slot],
            device_id=where,
            device_id_type=MESH,
        )

    home = gy + 3
    away = jnp.where(near_high, gy - 5, jnp.minimum(gy + 11, SLOTS - 1))
    away_x = jnp.where(near_high, gx_high, gx_low)

    def each_send(act):
        for k in range(1, GY):
            act(copy_f(k, 0, home, (sec, gx, lax.rem(gy + k, GY))))
        for k, y in enumerate((0, GY - 1)):
            act(copy_f(8 + k, 1, home, (other, gx, y)))

        @pl.when(near_edge)
        def _():
            for k in range(GY):
                act(copy_f(10 + k, 0, away, (sec, away_x, k)))
            for k, y in enumerate((0, GY - 1)):
                act(copy_f(18 + k, 1, away, (other, away_x, y)))

    each_send(lambda copy: copy.start())
    frac[0, home] = cf[...]
    for slot in range(SLOTS):

        @pl.when(slot != home)
        def _():
            copy_f(0, 0, slot, (sec, gx, lax.rem(gy + 1, GY))).wait_recv()

    @pl.when(at_end)
    def _():
        for slot in range(SLOTS):
            copy_f(0, 1, slot, (sec, gx, lax.rem(gy + 1, GY))).wait_recv()

    shift = lax.rem(COARSE + HALF - 32 * gy, COARSE)
    rows = SLOTS * 8
    mine = pltpu.roll(frac[0].reshape(rows, COARSE), shift, 1)[:, :TILE]
    beyond = pltpu.roll(frac[1].reshape(rows, COARSE), shift, 1)[:, :TILE]
    place = lanes((rows, TILE))
    from_other = ((place < HALF) & (gy == 0)) | ((place >= HALF + 32) & (gy == GY - 1))
    window = jnp.where(from_other, beyond, mine)
    j, i = sublanes((TILE, 32)), lanes((TILE, 32))
    band_y = ((j >= i) & (j < i + WIN)).astype(F32)
    i, m = sublanes((64, rows)), lanes((64, rows))
    which, i = i // 32, lax.rem(i, 32)
    at_row = (m // 8) * 4 + lax.rem(m, 4)
    band_x = ((lax.rem(m, 8) // 4 == which) & (at_row >= i) & (at_row < i + WIN)).astype(F32)
    sums = jnp.dot(window, band_y, precision=lax.Precision.HIGHEST, preferred_element_type=F32)
    area = jnp.dot(band_x, sums, precision=lax.Precision.HIGHEST, preferred_element_type=F32)
    area = area * (1.0 / (WIN * WIN))
    own = pltpu.roll(window, TILE - HALF, 1)
    for c in range(2):
        area_out[c] = area[32 * c : 32 * c + 32, :]
        for k in range(GY):
            at = 8 * (k + 3) + 4 * c
            column_out[c, 4 * k : 4 * k + 4, :] = own[at : at + 4, 0:32]

    for side in range(2):
        for f in range(FIELDS):
            copy_x(side, f).wait_send()
    for k in range(3):
        copy_p(k).wait_send()
    for k in range(1, GY):
        copy_l(k).wait_send()
    each_send(lambda copy: copy.wait_send())


def write_out(adv, column_fraction, area_fraction, out, column_out, area_out, sem):
    copies = [
        pltpu.make_async_copy(adv.at[f], out.at[f], sem.at[f]) for f in range(FIELDS)
    ] + [
        pltpu.make_async_copy(column_fraction, column_out, sem.at[FIELDS]),
        pltpu.make_async_copy(area_fraction, area_out, sem.at[FIELDS + 1]),
    ]
    for copy in copies:
        copy.start()
    for copy in copies:
        copy.wait()


def on_device(
    state, h_coeff, v_coeff, conv_weight, conv_bias, readout, readout_bias, level_base, level_depth
):
    vmem = pl.BlockSpec(memory_space=pltpu.VMEM)
    smem = pl.BlockSpec(memory_space=pltpu.SMEM)
    anywhere = pl.BlockSpec(memory_space=pl.ANY)
    dma = pltpu.SemaphoreType.DMA
    taps = KERNEL * KERNEL
    out, column_fraction, area_fraction = pl.pallas_call(
        kernel,
        out_shape=(
            pltpu.VMEM((FIELDS, ROWS, LEV, COLS), F32),
            pltpu.VMEM((2, 32, 32), F32),
            pltpu.VMEM((2, 32, 32), F32),
        ),
        in_specs=[anywhere, vmem, vmem, vmem, smem, smem, smem, vmem, vmem],
        out_specs=(vmem, vmem, vmem),
        scratch_shapes=[
            pltpu.VMEM((FIELDS, ROWS + 8, LEV, WIDE), F32),
            pltpu.VMEM((FIELDS, ROWS + 4, LEV, WIDE), F32),
            pltpu.VMEM((FIELDS, ROWS, LEV, COLS), BF16),
            pltpu.VMEM((FIELDS, 3, LEV, TILE), F32),
            pltpu.VMEM((2 * TILE, 2 * TILE), BF16),
            pltpu.VMEM((2, FIELDS, 4, LEV, COLS), BF16),
            pltpu.VMEM((2, FIELDS, 4, LEV, COLS), BF16),
            pltpu.VMEM((5, LEV, TILE), F32),
            pltpu.VMEM((7, LEV, TILE), F32),
            pltpu.VMEM((GY, 2, 8, TILE), F32),
            pltpu.VMEM((GY, 2, 8, TILE), F32),
            pltpu.VMEM((KERNEL * TILE, KERNEL * TILE), BF16),
            pltpu.VMEM((taps * FIELDS, CHANNELS), F32),
            pltpu.VMEM((CHANNELS * LEV, FIELDS * taps * LEV), BF16),
            pltpu.VMEM((2, 2, FIELDS * taps * LEV, COARSE), BF16),
            pltpu.VMEM((4, CHANNELS * LEV, COARSE), F32),
            pltpu.VMEM((8, COARSE), F32),
            pltpu.VMEM((2, SLOTS, 8, COARSE), F32),
            dma((3, FIELDS)),
            dma((2, FIELDS)),
            dma((2, FIELDS)),
            dma((3,)),
            dma((3,)),
            dma((GY,)),
            dma((GY,)),
            dma((20,)),
            dma((2, SLOTS)),
        ],
        compiler_params=pltpu.CompilerParams(
            collective_id=0, has_side_effects=True, vmem_limit_bytes=48 * 2**20
        ),
        name="steps_and_fractions",
    )(
        jnp.transpose(state, (0, 2, 1, 3)),
        h_coeff,
        v_coeff,
        jnp.transpose(conv_weight, (1, 2, 0, 3)),
        conv_bias,
        jnp.transpose(readout),
        readout_bias,
        level_base,
        level_depth,
    )
    out, column_fraction, area_fraction = pl.pallas_call(
        write_out,
        out_shape=(
            jax.ShapeDtypeStruct((FIELDS, ROWS, LEV, COLS), F32),
            jax.ShapeDtypeStruct((2, 32, 32), F32),
            jax.ShapeDtypeStruct((2, 32, 32), F32),
        ),
        in_specs=[vmem, vmem, vmem],
        out_specs=(anywhere, anywhere, anywhere),
        scratch_shapes=[dma((FIELDS + 2,))],
        compiler_params=pltpu.CompilerParams(vmem_limit_bytes=2**20),
        name="write_out",
    )(out, column_fraction, area_fraction)
    return jnp.transpose(out, (0, 2, 1, 3)), column_fraction, area_fraction


def solution(mesh):
    in_specs = (
        P(None, None, ("gx", "gy"), "sec"),
        P(),
        P(),
        P(),
        P(),
        P(),
        P(),
        P(None, "gx", ("sec", "gy")),
        P(None, "gx", ("sec", "gy")),
    )
    out_specs = (
        P(None, None, ("gx", "gy"), "sec"),
        P(None, "gx", ("sec", "gy")),
        P(None, "gx", ("sec", "gy")),
    )
    return jax.shard_map(
        on_device, mesh=mesh, in_specs=in_specs, out_specs=out_specs, check_vma=False
    )
```

```python
import jax
import jax.numpy as jnp
from jax import lax
from jax.experimental import pallas as pl
from jax.experimental.pallas import tpu as pltpu
from jax.sharding import PartitionSpec as P

F32 = jnp.float32
BF16 = jnp.bfloat16
MESH = pl.DeviceIdType.MESH

FIELDS = 4
LEV = 16
ROWS = 20
COLS = 1280
TILE = 128
TILES = COLS // TILE
KERNEL = 5
CHANNELS = 32
COARSE = 256
WIN = 24
HALF = WIN // 2
GY = 8
GX = 8
SLOTS = 14


def lanes(shape):
    return lax.broadcasted_iota(jnp.int32, shape, len(shape) - 1)


def sublanes(shape):
    return lax.broadcasted_iota(jnp.int32, shape, len(shape) - 2)


def stencil(src, ends, coef, band, f, rows, wanted, emit):
    lane = lanes((LEV, TILE))
    sub = sublanes((8, TILE))
    tiles = TILES + 1
    needed = sorted({(t + d) % tiles for t in wanted for d in (-1, 0, 1)})

    def at(r, t):
        if t == TILES:
            return ends[f, r]
        return src[f, r, :, TILE * t : TILE * t + TILE]

    parts = []
    for r in rows:
        for t in needed:
            value = at(r, t)
            head = value.astype(BF16)
            tail = (value - head.astype(F32)).astype(BF16)
            parts.append(jnp.concatenate([head, tail], axis=1))
    sums = jnp.dot(jnp.concatenate(parts, axis=0), band[...], preferred_element_type=F32)

    c0, c1, c2 = coef[f, 0], coef[f, 1], coef[f, 2]
    for q, r in enumerate(rows):

        def along_y(t, part):
            first = LEV * (q * len(needed) + needed.index(t % tiles))
            return sums[first : first + LEV, TILE * part : TILE * part + TILE]

        for t in wanted:
            value = at(r, t)
            y = along_y(t, 0) + jnp.where(lane < 64, along_y(t - 1, 1), along_y(t + 1, 1))
            low, high = value[:8], value[8:]
            low_down, high_down = pltpu.roll(low, 1, 0), pltpu.roll(high, 1, 0)
            low_up, high_up = pltpu.roll(low, 7, 0), pltpu.roll(high, 7, 0)
            vert = jnp.concatenate(
                [
                    jnp.where(sub == 0, 0.0, low_down) + jnp.where(sub == 7, high_up, low_up),
                    jnp.where(sub == 0, low_down, high_down) + jnp.where(sub == 7, 0.0, high_up),
                ],
                axis=0,
            )
            x = 16.0 * (at(r - 1, t) + at(r + 1, t)) - (at(r - 2, t) + at(r + 2, t))
            emit(r, t, (c0 * value + c1 * (x + y)) + c2 * vert)


def kernel(
    state,
    h_coeff,
    v_coeff,
    weight,
    conv_bias,
    readout,
    readout_bias,
    level_base,
    level_depth,
    adv,
    column_out,
    area_out,
    st,
    st_ends,
    u,
    u_ends,
    ab,
    coef,
    band,
    send_x,
    recv_x,
    send_p,
    recv_p,
    send_l,
    recv_l,
    select,
    taps_w,
    conv_l,
    dmat,
    feat,
    cf,
    frac,
    load_sem,
    sx_sem,
    rx_sem,
    sp_sem,
    rp_sem,
    sl_sem,
    rl_sem,
    sf_sem,
    rf_sem,
):
    sec, gx, gy = lax.axis_index("sec"), lax.axis_index("gx"), lax.axis_index("gy")
    other = 1 - sec
    gx_low, gx_high = lax.rem(gx + GX - 1, GX), lax.rem(gx + 1, GX)
    brick = gx * GY + gy
    low, high = lax.rem(brick + GX * GY - 1, GX * GY), lax.rem(brick + 1, GX * GY)
    low_x, low_y, high_x, high_y = low // GY, lax.rem(low, GY), high // GY, lax.rem(high, GY)
    near_low, near_high = gy <= 2, gy >= 5
    near_edge = near_low | near_high
    at_end = (gy == 0) | (gy == GY - 1)

    spans = ((0, 4), (16, 4), (4, 12))
    loads = []
    for part, (first, count) in enumerate(spans):
        for f in range(FIELDS):
            copy = pltpu.make_async_copy(
                state.at[f, pl.ds(first, count)],
                st.at[f, pl.ds(first + 4, count)],
                load_sem.at[part, f],
            )
            copy.start()
            loads.append(copy)

    barrier = pltpu.get_barrier_semaphore()

    def hello(where):
        pl.semaphore_signal(barrier, inc=1, device_id=where, device_id_type=MESH)

    hello((sec, low_x, low_y))
    hello((sec, high_x, high_y))
    hello((other, gx, gy))
    hello((other, low_x, low_y))
    hello((other, high_x, high_y))
    for k in range(1, GY):
        hello((sec, gx, lax.rem(gy + k, GY)))
    for k in range(3):
        hello((sec, gx_high, k))
        hello((sec, gx_low, 5 + k))

    @pl.when(at_end)
    def _():
        for k in range(GY):
            hello((other, gx, k))
        for k in range(3):
            hello((other, gx_high, k))
            hello((other, gx_low, 5 + k))

    for copy in loads[: 2 * FIELDS]:
        copy.wait()

    lane = lanes((LEV, TILE))
    group_of = lax.rem(lane + 4, TILE) // 8

    @pl.loop(0, FIELDS)
    def _(f):
        for side, first in enumerate((4, 20)):
            for row in range(4):
                send_x[side, f, row] = st[f, first + row].astype(BF16)

    pl.semaphore_wait(barrier, 14 + jnp.where(near_edge, 10, 0))

    def copy_x(side, f):
        where = (sec, low_x, low_y) if side == 0 else (sec, high_x, high_y)
        return pltpu.make_async_remote_copy(
            send_x.at[side, f],
            recv_x.at[1 - side, f],
            sx_sem.at[side, f],
            rx_sem.at[1 - side, f],
            device_id=where,
            device_id_type=MESH,
        )

    def copy_p(k):
        source, target, where = (
            (send_p, recv_p.at[pl.ds(1, 5)], (other, gx, gy)),
            (send_p.at[0:1], recv_p.at[pl.ds(6, 1)], (other, low_x, low_y)),
            (send_p.at[4:5], recv_p.at[pl.ds(0, 1)], (other, high_x, high_y)),
        )[k]
        return pltpu.make_async_remote_copy(
            source, target, sp_sem.at[k], rp_sem.at[k], device_id=where, device_id_type=MESH
        )

    def copy_l(k):
        to = lax.rem(gy + k, GY)
        return pltpu.make_async_remote_copy(
            send_l.at[to],
            recv_l.at[gy],
            sl_sem.at[k],
            rl_sem.at[gy],
            device_id=(sec, gx, to),
            device_id_type=MESH,
        )

    for f in range(FIELDS):
        copy_x(0, f).start()
        copy_x(1, f).start()

    def edge(f, row):
        return jnp.where(lane < 64, st[f, row, :, :TILE], st[f, row, :, COLS - TILE : COLS])

    def pack(group):
        total = jnp.zeros((LEV, TILE), F32)
        for j in range(16):
            part = pltpu.roll(edge(j // 4, 4 + 4 * group + j % 4), 8 * j, 1)
            total = jnp.where(group_of == j, part, total)
        send_p[group] = total

    for copy in loads[2 * FIELDS :]:
        copy.wait()
    for group in range(5):
        pack(group)

    for k in range(3):
        copy_p(k).start()

    eye = (sublanes((LEV, LEV)) == lanes((LEV, LEV))).astype(F32)
    for f in range(FIELDS):
        horiz = jnp.sum(eye * h_coeff[f : f + 1, :], axis=1, keepdims=True)
        vertical = jnp.sum(eye * v_coeff[f : f + 1, :], axis=1, keepdims=True)
        for k, value in enumerate(
            (
                1.0 - 5.0 * horiz - 2.0 * vertical,
                horiz * (1.0 / 12.0),
                vertical,
            )
        ):
            coef[f, k] = jnp.broadcast_to(value, (LEV, TILE))

    i, j = sublanes((2 * TILE, 2 * TILE)), lanes((2 * TILE, 2 * TILE))
    away = jnp.abs(lax.rem(i, TILE) - lax.rem(j, TILE))
    away = jnp.where(j < TILE, away, TILE - away)
    taps_y = jnp.where(away == 1, 16.0, jnp.where(away == 2, -1.0, 0.0))
    band[...] = taps_y.astype(BF16)


    send_l[...] = jnp.zeros_like(send_l)
    for k in range(GY):
        for c in range(2):
            for kind, ref in enumerate((level_base, level_depth)):
                send_l[k, kind, 4 * c : 4 * c + 4, 0:32] = ref[c, 4 * k : 4 * k + 4, :].astype(F32)
    turn = 32 * lax.rem(gy, 4)
    for k in range(GY):
        for kind in range(2):
            send_l[k, kind] = pltpu.roll(send_l[k, kind], turn, 1)
    for k in range(1, GY):
        copy_l(k).start()
    recv_l[gy] = send_l[gy]

    row = sublanes((KERNEL * TILE, TILE))
    col = lanes((KERNEL * TILE, TILE))
    for b in range(KERNEL):
        select[:, TILE * b : TILE * b + TILE] = (row == KERNEL * col + b).astype(F32).astype(BF16)
    taps = KERNEL * KERNEL
    for tap in range(taps):
        taps_w[FIELDS * tap : FIELDS * tap + FIELDS, :] = weight[tap // KERNEL, tap % KERNEL].astype(F32)
    shape = (CHANNELS * LEV, CHANNELS)
    spread = (sublanes(shape) // LEV == lanes(shape)).astype(F32).astype(BF16)
    wide_w = lax.dot_general(
        spread,
        taps_w[...].astype(BF16),
        (((1,), (1,)), ((), ())),
        preferred_element_type=F32,
    ).astype(BF16)
    shape = (taps * FIELDS, FIELDS * taps * LEV)
    tap_at = lanes(shape) // LEV
    pick = (sublanes(shape) == lax.rem(tap_at, taps) * FIELDS + tap_at // taps).astype(F32)
    full = jnp.dot(wide_w, pick.astype(BF16), preferred_element_type=F32)
    same = lax.rem(sublanes(full.shape), LEV) == lax.rem(lanes(full.shape), LEV)
    conv_l[...] = jnp.where(same, full, 0.0).astype(BF16)

    def unpack(group):
        for j in range(16):
            st_ends[j // 4, 4 * group + j % 4] = pltpu.roll(
                recv_p[group], (TILE - 8 * j) % TILE, 1
            )

    @pl.loop(0, FIELDS)
    def _(f):
        for r in range(4, ROWS + 4):
            st_ends[f, r] = jnp.zeros((LEV, TILE), F32)

    def first_step(f, rows, wanted=range(TILES + 1)):
        def emit(r, t, value):
            if t == TILES:
                u_ends[f, r - 2] = value
            else:
                u[f, r - 2, :, TILE * t : TILE * t + TILE] = value

        stencil(st, st_ends, coef, band, f, rows, wanted, emit)

    def second_step(f, rows, wanted=range(TILES)):
        def emit(r, t, value):
            adv[f, r - 2, :, TILE * t : TILE * t + TILE] = value
            ab[f, r - 2, :, TILE * t : TILE * t + TILE] = value.astype(BF16)

        stencil(u, u_ends, coef, band, f, rows, wanted, emit)

    @pl.loop(0, FIELDS)
    def _(f):
        first_step(f, range(6, 14))
        first_step(f, range(14, 22))
        second_step(f, range(6, 18))

    def take(f, pair, slot):
        blocks = [
            ab[f, KERNEL * p : KERNEL * p + KERNEL, :, 640 * half : 640 * half + 640].reshape(
                KERNEL * LEV, KERNEL * TILE
            )
            for p in pair
            for half in range(2)
        ]
        taken = jnp.dot(
            jnp.concatenate(blocks, axis=0), select[...], preferred_element_type=F32
        ).astype(BF16)
        for i in range(2):
            for half in range(2):
                for a in range(KERNEL):
                    first = LEV * (KERNEL * (2 * i + half) + a)
                    for b in range(KERNEL):
                        tap = LEV * (taps * f + KERNEL * a + b)
                        dmat[slot, i, tap : tap + LEV, TILE * half : TILE * half + TILE] = taken[
                            first : first + LEV, TILE * b : TILE * b + TILE
                        ]

    copy_p(0).wait_recv()
    for group in range(1, 6):
        unpack(group)

    @pl.loop(0, FIELDS)
    def _(f):
        first_step(f, range(6, 22), (TILES - 1, TILES, 0))
        second_step(f, range(6, 18), (TILES - 1, 0))

    for f in range(FIELDS):
        take(f, (1, 2), 0)
    for i, p in enumerate((1, 2)):
        feat[p] = jnp.dot(conv_l[...], dmat[0, i], preferred_element_type=F32)

    for k in range(1, 3):
        copy_p(k).wait_recv()
    unpack(0)
    unpack(6)
    early = 9 * TILE
    for f in range(FIELDS):
        copy_x(0, f).wait_recv()
        copy_x(1, f).wait_recv()
        for side, first in enumerate((0, 24)):
            for row in range(4):
                st[f, first + row] = recv_x[side, f, row].astype(F32)

        first_step(f, (2, 3, 4, 5, 22, 23, 24, 25))
        second_step(f, (2, 3, 4, 5, 18, 19, 20, 21))
        take(f, (0, 3), 1)
        if f == 2:
            for i, p in enumerate((0, 3)):
                feat[p] = jnp.dot(
                    conv_l[:, :early], dmat[1, i, :early], preferred_element_type=F32
                )
    for i, p in enumerate((0, 3)):
        feat[p] += jnp.dot(conv_l[:, early:], dmat[1, i, early:], preferred_element_type=F32)

    for k in range(1, GY):
        pltpu.make_async_remote_copy(
            send_l.at[0],
            recv_l.at[lax.rem(gy + k, GY)],
            sl_sem.at[k],
            rl_sem.at[lax.rem(gy + k, GY)],
            device_id=(sec, gx, lax.rem(gy + k, GY)),
            device_id_type=MESH,
        ).wait_recv()
    base, depth = (
        jnp.concatenate(
            [
                (recv_l[4 * t, kind] + recv_l[4 * t + 1, kind])
                + (recv_l[4 * t + 2, kind] + recv_l[4 * t + 3, kind])
                for t in range(2)
            ],
            axis=1,
        )
        for kind in range(2)
    )
    level = sublanes((LEV, COARSE)).astype(F32)
    for p in range(4):
        score = [jnp.zeros((LEV, COARSE), F32) for _ in range(2)]
        for k in range(CHANNELS):
            value = jnp.maximum(feat[p, LEV * k : LEV * k + LEV, :] + conv_bias[k], 0.0)
            for c in range(2):
                score[c] = score[c] + readout[c, k] * value
        for c in range(2):
            prob = jax.nn.sigmoid(score[c] + readout_bias[c])
            at = 4 * c + p
            least, many = base[at : at + 1, :], depth[at : at + 1, :]
            inside = (level >= least) & (level < least + many)
            total = jnp.sum(jnp.where(inside, prob, 0.0), axis=0, keepdims=True)
            cf[at : at + 1, :] = total / many

    def copy_f(index, which, slot, where):
        return pltpu.make_async_remote_copy(
            cf,
            frac.at[which, slot],
            sf_sem.at[index],
            rf_sem.at[which, slot],
            device_id=where,
            device_id_type=MESH,
        )

    home = gy + 3
    away = jnp.where(near_high, gy - 5, jnp.minimum(gy + 11, SLOTS - 1))
    away_x = jnp.where(near_high, gx_high, gx_low)

    def each_send(act):
        for k in range(1, GY):
            act(copy_f(k, 0, home, (sec, gx, lax.rem(gy + k, GY))))
        for k, y in enumerate((0, GY - 1)):
            act(copy_f(8 + k, 1, home, (other, gx, y)))

        @pl.when(near_edge)
        def _():
            for k in range(GY):
                act(copy_f(10 + k, 0, away, (sec, away_x, k)))
            for k, y in enumerate((0, GY - 1)):
                act(copy_f(18 + k, 1, away, (other, away_x, y)))

    each_send(lambda copy: copy.start())
    frac[0, home] = cf[...]
    for slot in range(SLOTS):

        @pl.when(slot != home)
        def _():
            copy_f(0, 0, slot, (sec, gx, lax.rem(gy + 1, GY))).wait_recv()

    @pl.when(at_end)
    def _():
        for slot in range(SLOTS):
            copy_f(0, 1, slot, (sec, gx, lax.rem(gy + 1, GY))).wait_recv()

    shift = lax.rem(COARSE + HALF - 32 * gy, COARSE)
    rows = SLOTS * 8
    mine = pltpu.roll(frac[0].reshape(rows, COARSE), shift, 1)[:, :TILE]
    beyond = pltpu.roll(frac[1].reshape(rows, COARSE), shift, 1)[:, :TILE]
    place = lanes((rows, TILE))
    from_other = ((place < HALF) & (gy == 0)) | ((place >= HALF + 32) & (gy == GY - 1))
    window = jnp.where(from_other, beyond, mine)
    j, i = sublanes((TILE, 32)), lanes((TILE, 32))
    band_y = ((j >= i) & (j < i + WIN)).astype(F32)
    i, m = sublanes((64, rows)), lanes((64, rows))
    which, i = i // 32, lax.rem(i, 32)
    at_row = (m // 8) * 4 + lax.rem(m, 4)
    band_x = ((lax.rem(m, 8) // 4 == which) & (at_row >= i) & (at_row < i + WIN)).astype(F32)
    sums = jnp.dot(window, band_y, precision=lax.Precision.HIGHEST, preferred_element_type=F32)
    area = jnp.dot(band_x, sums, precision=lax.Precision.HIGHEST, preferred_element_type=F32)
    area = area * (1.0 / (WIN * WIN))
    own = pltpu.roll(window, TILE - HALF, 1)
    for c in range(2):
        area_out[c] = area[32 * c : 32 * c + 32, :]
        for k in range(GY):
            at = 8 * (k + 3) + 4 * c
            column_out[c, 4 * k : 4 * k + 4, :] = own[at : at + 4, 0:32]

    for side in range(2):
        for f in range(FIELDS):
            copy_x(side, f).wait_send()
    for k in range(3):
        copy_p(k).wait_send()
    for k in range(1, GY):
        copy_l(k).wait_send()
    each_send(lambda copy: copy.wait_send())


def write_out(adv, column_fraction, area_fraction, out, column_out, area_out, sem):
    copies = [
        pltpu.make_async_copy(adv.at[f], out.at[f], sem.at[f]) for f in range(FIELDS)
    ] + [
        pltpu.make_async_copy(column_fraction, column_out, sem.at[FIELDS]),
        pltpu.make_async_copy(area_fraction, area_out, sem.at[FIELDS + 1]),
    ]
    for copy in copies:
        copy.start()
    for copy in copies:
        copy.wait()


def on_device(
    state, h_coeff, v_coeff, conv_weight, conv_bias, readout, readout_bias, level_base, level_depth
):
    vmem = pl.BlockSpec(memory_space=pltpu.VMEM)
    smem = pl.BlockSpec(memory_space=pltpu.SMEM)
    anywhere = pl.BlockSpec(memory_space=pl.ANY)
    dma = pltpu.SemaphoreType.DMA
    taps = KERNEL * KERNEL
    out, column_fraction, area_fraction = pl.pallas_call(
        kernel,
        out_shape=(
            pltpu.VMEM((FIELDS, ROWS, LEV, COLS), F32),
            pltpu.VMEM((2, 32, 32), F32),
            pltpu.VMEM((2, 32, 32), F32),
        ),
        in_specs=[anywhere, vmem, vmem, vmem, smem, smem, smem, vmem, vmem],
        out_specs=(vmem, vmem, vmem),
        scratch_shapes=[
            pltpu.VMEM((FIELDS, ROWS + 8, LEV, COLS), F32),
            pltpu.VMEM((FIELDS, ROWS + 8, LEV, TILE), F32),
            pltpu.VMEM((FIELDS, ROWS + 4, LEV, COLS), F32),
            pltpu.VMEM((FIELDS, ROWS + 4, LEV, TILE), F32),
            pltpu.VMEM((FIELDS, ROWS, LEV, COLS), BF16),
            pltpu.VMEM((FIELDS, 3, LEV, TILE), F32),
            pltpu.VMEM((2 * TILE, 2 * TILE), BF16),
            pltpu.VMEM((2, FIELDS, 4, LEV, COLS), BF16),
            pltpu.VMEM((2, FIELDS, 4, LEV, COLS), BF16),
            pltpu.VMEM((5, LEV, TILE), F32),
            pltpu.VMEM((7, LEV, TILE), F32),
            pltpu.VMEM((GY, 2, 8, TILE), F32),
            pltpu.VMEM((GY, 2, 8, TILE), F32),
            pltpu.VMEM((KERNEL * TILE, KERNEL * TILE), BF16),
            pltpu.VMEM((taps * FIELDS, CHANNELS), F32),
            pltpu.VMEM((CHANNELS * LEV, FIELDS * taps * LEV), BF16),
            pltpu.VMEM((2, 2, FIELDS * taps * LEV, COARSE), BF16),
            pltpu.VMEM((4, CHANNELS * LEV, COARSE), F32),
            pltpu.VMEM((8, COARSE), F32),
            pltpu.VMEM((2, SLOTS, 8, COARSE), F32),
            dma((3, FIELDS)),
            dma((2, FIELDS)),
            dma((2, FIELDS)),
            dma((3,)),
            dma((3,)),
            dma((GY,)),
            dma((GY,)),
            dma((20,)),
            dma((2, SLOTS)),
        ],
        compiler_params=pltpu.CompilerParams(
            collective_id=0, has_side_effects=True, vmem_limit_bytes=48 * 2**20
        ),
        name="steps_and_fractions",
    )(
        jnp.transpose(state, (0, 2, 1, 3)),
        h_coeff,
        v_coeff,
        jnp.transpose(conv_weight, (1, 2, 0, 3)),
        conv_bias,
        jnp.transpose(readout),
        readout_bias,
        level_base,
        level_depth,
    )
    out, column_fraction, area_fraction = pl.pallas_call(
        write_out,
        out_shape=(
            jax.ShapeDtypeStruct((FIELDS, ROWS, LEV, COLS), F32),
            jax.ShapeDtypeStruct((2, 32, 32), F32),
            jax.ShapeDtypeStruct((2, 32, 32), F32),
        ),
        in_specs=[vmem, vmem, vmem],
        out_specs=(anywhere, anywhere, anywhere),
        scratch_shapes=[dma((FIELDS + 2,))],
        compiler_params=pltpu.CompilerParams(vmem_limit_bytes=2**20),
        name="write_out",
    )(out, column_fraction, area_fraction)
    return jnp.transpose(out, (0, 2, 1, 3)), column_fraction, area_fraction


def solution(mesh):
    in_specs = (
        P(None, None, ("gx", "gy"), "sec"),
        P(),
        P(),
        P(),
        P(),
        P(),
        P(),
        P(None, "gx", ("sec", "gy")),
        P(None, "gx", ("sec", "gy")),
    )
    out_specs = (
        P(None, None, ("gx", "gy"), "sec"),
        P(None, "gx", ("sec", "gy")),
        P(None, "gx", ("sec", "gy")),
    )
    return jax.shard_map(
        on_device, mesh=mesh, in_specs=in_specs, out_specs=out_specs, check_vma=False
    )
```

```python
import jax
import jax.numpy as jnp
from jax import lax
from jax.experimental import pallas as pl
from jax.experimental.pallas import tpu as pltpu
from jax.sharding import PartitionSpec as P

F32 = jnp.float32
BF16 = jnp.bfloat16
MESH = pl.DeviceIdType.MESH

FIELDS = 4
LEV = 16
ROWS = 20
COLS = 1280
TILE = 128
TILES = COLS // TILE
WIDE = COLS + TILE
KERNEL = 5
CHANNELS = 32
COARSE = 256
WIN = 24
HALF = WIN // 2
GY = 8
GX = 8
SLOTS = 14


def lanes(shape):
    return lax.broadcasted_iota(jnp.int32, shape, len(shape) - 1)


def sublanes(shape):
    return lax.broadcasted_iota(jnp.int32, shape, len(shape) - 2)


def stencil(src, coef, band, f, rows, wanted, emit):
    lane = lanes((LEV, TILE))
    sub = sublanes((8, TILE))
    tiles = TILES + 1
    needed = sorted({(t + d) % tiles for t in wanted for d in (-1, 0, 1)})

    def at(r, t):
        return src[f, r, :, TILE * t : TILE * t + TILE]

    parts = []
    for r in rows:
        for t in needed:
            value = at(r, t)
            head = value.astype(BF16)
            tail = (value - head.astype(F32)).astype(BF16)
            parts.append(jnp.concatenate([head, tail], axis=1))
    sums = jnp.dot(jnp.concatenate(parts, axis=0), band[...], preferred_element_type=F32)

    c0, c1, c2 = coef[f, 0], coef[f, 1], coef[f, 2]
    for q, r in enumerate(rows):

        def along_y(t, part):
            first = LEV * (q * len(needed) + needed.index(t % tiles))
            return sums[first : first + LEV, TILE * part : TILE * part + TILE]

        for t in wanted:
            value = at(r, t)
            y = along_y(t, 0) + jnp.where(lane < 64, along_y(t - 1, 1), along_y(t + 1, 1))
            low, high = value[:8], value[8:]
            low_down, high_down = pltpu.roll(low, 1, 0), pltpu.roll(high, 1, 0)
            low_up, high_up = pltpu.roll(low, 7, 0), pltpu.roll(high, 7, 0)
            vert = jnp.concatenate(
                [
                    jnp.where(sub == 0, 0.0, low_down) + jnp.where(sub == 7, high_up, low_up),
                    jnp.where(sub == 0, low_down, high_down) + jnp.where(sub == 7, 0.0, high_up),
                ],
                axis=0,
            )
            x = 16.0 * (at(r - 1, t) + at(r + 1, t)) - (at(r - 2, t) + at(r + 2, t))
            emit(r, t, (c0 * value + c1 * (x + y)) + c2 * vert)


def kernel(
    state,
    h_coeff,
    v_coeff,
    weight,
    conv_bias,
    readout,
    readout_bias,
    level_base,
    level_depth,
    adv,
    column_out,
    area_out,
    st,
    u,
    ab,
    coef,
    band,
    send_x,
    recv_x,
    send_p,
    recv_p,
    send_l,
    recv_l,
    select,
    taps_w,
    conv_l,
    dmat,
    feat,
    cf,
    frac,
    load_sem,
    sx_sem,
    rx_sem,
    sp_sem,
    rp_sem,
    sl_sem,
    rl_sem,
    sf_sem,
    rf_sem,
):
    sec, gx, gy = lax.axis_index("sec"), lax.axis_index("gx"), lax.axis_index("gy")
    other = 1 - sec
    gx_low, gx_high = lax.rem(gx + GX - 1, GX), lax.rem(gx + 1, GX)
    brick = gx * GY + gy
    low, high = lax.rem(brick + GX * GY - 1, GX * GY), lax.rem(brick + 1, GX * GY)
    low_x, low_y, high_x, high_y = low // GY, lax.rem(low, GY), high // GY, lax.rem(high, GY)
    near_low, near_high = gy <= 2, gy >= 5
    near_edge = near_low | near_high
    at_end = (gy == 0) | (gy == GY - 1)

    spans = ((0, 4), (16, 4), (4, 12))
    loads = []
    for part, (first, count) in enumerate(spans):
        for f in range(FIELDS):
            copy = pltpu.make_async_copy(
                state.at[f, pl.ds(first, count)],
                st.at[f, pl.ds(first + 4, count), :, pl.ds(0, COLS)],
                load_sem.at[part, f],
            )
            copy.start()
            loads.append(copy)

    barrier = pltpu.get_barrier_semaphore()

    def hello(where):
        pl.semaphore_signal(barrier, inc=1, device_id=where, device_id_type=MESH)

    hello((sec, low_x, low_y))
    hello((sec, high_x, high_y))
    hello((other, gx, gy))
    hello((other, low_x, low_y))
    hello((other, high_x, high_y))
    for k in range(1, GY):
        hello((sec, gx, lax.rem(gy + k, GY)))
    for k in range(3):
        hello((sec, gx_high, k))
        hello((sec, gx_low, 5 + k))

    @pl.when(at_end)
    def _():
        for k in range(GY):
            hello((other, gx, k))
        for k in range(3):
            hello((other, gx_high, k))
            hello((other, gx_low, 5 + k))

    for copy in loads[: 2 * FIELDS]:
        copy.wait()

    lane = lanes((LEV, TILE))
    group_of = lax.rem(lane + 4, TILE) // 8

    @pl.loop(0, FIELDS)
    def _(f):
        for side, first in enumerate((4, 20)):
            for row in range(4):
                send_x[side, f, row] = st[f, first + row, :, :COLS].astype(BF16)

    pl.semaphore_wait(barrier, 14 + jnp.where(near_edge, 10, 0))

    def copy_x(side, f):
        where = (sec, low_x, low_y) if side == 0 else (sec, high_x, high_y)
        return pltpu.make_async_remote_copy(
            send_x.at[side, f],
            recv_x.at[1 - side, f],
            sx_sem.at[side, f],
            rx_sem.at[1 - side, f],
            device_id=where,
            device_id_type=MESH,
        )

    def copy_p(k):
        source, target, where = (
            (send_p, recv_p.at[pl.ds(1, 5)], (other, gx, gy)),
            (send_p.at[0:1], recv_p.at[pl.ds(6, 1)], (other, low_x, low_y)),
            (send_p.at[4:5], recv_p.at[pl.ds(0, 1)], (other, high_x, high_y)),
        )[k]
        return pltpu.make_async_remote_copy(
            source, target, sp_sem.at[k], rp_sem.at[k], device_id=where, device_id_type=MESH
        )

    def copy_l(k):
        to = lax.rem(gy + k, GY)
        return pltpu.make_async_remote_copy(
            send_l.at[to],
            recv_l.at[gy],
            sl_sem.at[k],
            rl_sem.at[gy],
            device_id=(sec, gx, to),
            device_id_type=MESH,
        )

    for f in range(FIELDS):
        copy_x(0, f).start()
        copy_x(1, f).start()

    def edge(f, row):
        return jnp.where(lane < 64, st[f, row, :, :TILE], st[f, row, :, COLS - TILE : COLS])

    def pack(group):
        total = jnp.zeros((LEV, TILE), F32)
        for j in range(16):
            part = pltpu.roll(edge(j // 4, 4 + 4 * group + j % 4), 8 * j, 1)
            total = jnp.where(group_of == j, part, total)
        send_p[group] = total

    for copy in loads[2 * FIELDS :]:
        copy.wait()
    for group in range(5):
        pack(group)

    for k in range(3):
        copy_p(k).start()

    eye = (sublanes((LEV, LEV)) == lanes((LEV, LEV))).astype(F32)
    for f in range(FIELDS):
        horiz = jnp.sum(eye * h_coeff[f : f + 1, :], axis=1, keepdims=True)
        vertical = jnp.sum(eye * v_coeff[f : f + 1, :], axis=1, keepdims=True)
        for k, value in enumerate(
            (
                1.0 - 5.0 * horiz - 2.0 * vertical,
                horiz * (1.0 / 12.0),
                vertical,
            )
        ):
            coef[f, k] = jnp.broadcast_to(value, (LEV, TILE))

    i, j = sublanes((2 * TILE, 2 * TILE)), lanes((2 * TILE, 2 * TILE))
    away = jnp.abs(lax.rem(i, TILE) - lax.rem(j, TILE))
    away = jnp.where(j < TILE, away, TILE - away)
    taps_y = jnp.where(away == 1, 16.0, jnp.where(away == 2, -1.0, 0.0))
    band[...] = taps_y.astype(BF16)


    send_l[...] = jnp.zeros_like(send_l)
    for k in range(GY):
        for c in range(2):
            for kind, ref in enumerate((level_base, level_depth)):
                send_l[k, kind, 4 * c : 4 * c + 4, 0:32] = ref[c, 4 * k : 4 * k + 4, :].astype(F32)
    turn = 32 * lax.rem(gy, 4)
    for k in range(GY):
        for kind in range(2):
            send_l[k, kind] = pltpu.roll(send_l[k, kind], turn, 1)
    for k in range(1, GY):
        copy_l(k).start()
    recv_l[gy] = send_l[gy]

    row = sublanes((KERNEL * TILE, TILE))
    col = lanes((KERNEL * TILE, TILE))
    for b in range(KERNEL):
        select[:, TILE * b : TILE * b + TILE] = (row == KERNEL * col + b).astype(F32).astype(BF16)
    taps = KERNEL * KERNEL
    for tap in range(taps):
        taps_w[FIELDS * tap : FIELDS * tap + FIELDS, :] = weight[tap // KERNEL, tap % KERNEL].astype(F32)
    shape = (CHANNELS * LEV, CHANNELS)
    spread = (sublanes(shape) // LEV == lanes(shape)).astype(F32).astype(BF16)
    wide_w = lax.dot_general(
        spread,
        taps_w[...].astype(BF16),
        (((1,), (1,)), ((), ())),
        preferred_element_type=F32,
    ).astype(BF16)
    shape = (taps * FIELDS, FIELDS * taps * LEV)
    tap_at = lanes(shape) // LEV
    pick = (sublanes(shape) == lax.rem(tap_at, taps) * FIELDS + tap_at // taps).astype(F32)
    full = jnp.dot(wide_w, pick.astype(BF16), preferred_element_type=F32)
    same = lax.rem(sublanes(full.shape), LEV) == lax.rem(lanes(full.shape), LEV)
    conv_l[...] = jnp.where(same, full, 0.0).astype(BF16)

    def unpack(group):
        for j in range(16):
            st[j // 4, 4 * group + j % 4, :, COLS:] = pltpu.roll(
                recv_p[group], (TILE - 8 * j) % TILE, 1
            )

    @pl.loop(0, FIELDS)
    def _(f):
        for r in range(ROWS + 8):
            st[f, r, :, COLS:] = jnp.zeros((LEV, TILE), F32)

    def first_step(f, rows, wanted=range(TILES + 1)):
        def emit(r, t, value):
            u[f, r - 2, :, TILE * t : TILE * t + TILE] = value

        stencil(st, coef, band, f, rows, wanted, emit)

    def second_step(f, rows, wanted=range(TILES)):
        def emit(r, t, value):
            adv[f, r - 2, :, TILE * t : TILE * t + TILE] = value
            ab[f, r - 2, :, TILE * t : TILE * t + TILE] = value.astype(BF16)

        stencil(u, coef, band, f, rows, wanted, emit)

    @pl.loop(0, FIELDS)
    def _(f):
        first_step(f, range(6, 14))
        first_step(f, range(14, 22))
        second_step(f, range(6, 18))

    def take(f, pair, slot):
        blocks = [
            ab[f, KERNEL * p : KERNEL * p + KERNEL, :, 640 * half : 640 * half + 640].reshape(
                KERNEL * LEV, KERNEL * TILE
            )
            for p in pair
            for half in range(2)
        ]
        taken = jnp.dot(
            jnp.concatenate(blocks, axis=0), select[...], preferred_element_type=F32
        ).astype(BF16)
        for i in range(2):
            for half in range(2):
                for a in range(KERNEL):
                    first = LEV * (KERNEL * (2 * i + half) + a)
                    for b in range(KERNEL):
                        tap = LEV * (taps * f + KERNEL * a + b)
                        dmat[slot, i, tap : tap + LEV, TILE * half : TILE * half + TILE] = taken[
                            first : first + LEV, TILE * b : TILE * b + TILE
                        ]

    for f in range(FIELDS):
        copy_x(0, f).wait_recv()
        copy_x(1, f).wait_recv()
        for side, first in enumerate((0, 24)):
            for row in range(4):
                st[f, first + row, :, :COLS] = recv_x[side, f, row].astype(F32)

        first_step(f, (2, 3, 4, 5, 22, 23, 24, 25))
        second_step(f, (2, 3, 4, 5, 18, 19, 20, 21))

    for k in range(3):
        copy_p(k).wait_recv()
    for group in range(7):
        unpack(group)

    @pl.loop(0, FIELDS)
    def _(f):
        first_step(f, range(2, 26), (TILES - 1, TILES, 0))
        second_step(f, range(2, 22), (TILES - 1, 0))

    for slot, pair in enumerate(((1, 2), (0, 3))):
        for f in range(FIELDS):
            take(f, pair, slot)
        for i, p in enumerate(pair):
            feat[p] = jnp.dot(conv_l[...], dmat[slot, i], preferred_element_type=F32)

    for k in range(1, GY):
        pltpu.make_async_remote_copy(
            send_l.at[0],
            recv_l.at[lax.rem(gy + k, GY)],
            sl_sem.at[k],
            rl_sem.at[lax.rem(gy + k, GY)],
            device_id=(sec, gx, lax.rem(gy + k, GY)),
            device_id_type=MESH,
        ).wait_recv()
    base, depth = (
        jnp.concatenate(
            [
                (recv_l[4 * t, kind] + recv_l[4 * t + 1, kind])
                + (recv_l[4 * t + 2, kind] + recv_l[4 * t + 3, kind])
                for t in range(2)
            ],
            axis=1,
        )
        for kind in range(2)
    )
    level = sublanes((LEV, COARSE)).astype(F32)
    for p in range(4):
        score = [jnp.zeros((LEV, COARSE), F32) for _ in range(2)]
        for k in range(CHANNELS):
            value = jnp.maximum(feat[p, LEV * k : LEV * k + LEV, :] + conv_bias[k], 0.0)
            for c in range(2):
                score[c] = score[c] + readout[c, k] * value
        for c in range(2):
            prob = jax.nn.sigmoid(score[c] + readout_bias[c])
            at = 4 * c + p
            least, many = base[at : at + 1, :], depth[at : at + 1, :]
            inside = (level >= least) & (level < least + many)
            total = jnp.sum(jnp.where(inside, prob, 0.0), axis=0, keepdims=True)
            cf[at : at + 1, :] = total / many

    def copy_f(index, which, slot, where):
        return pltpu.make_async_remote_copy(
            cf,
            frac.at[which, slot],
            sf_sem.at[index],
            rf_sem.at[which, slot],
            device_id=where,
            device_id_type=MESH,
        )

    home = gy + 3
    away = jnp.where(near_high, gy - 5, jnp.minimum(gy + 11, SLOTS - 1))
    away_x = jnp.where(near_high, gx_high, gx_low)

    def each_send(act):
        for k in range(1, GY):
            act(copy_f(k, 0, home, (sec, gx, lax.rem(gy + k, GY))))
        for k, y in enumerate((0, GY - 1)):
            act(copy_f(8 + k, 1, home, (other, gx, y)))

        @pl.when(near_edge)
        def _():
            for k in range(GY):
                act(copy_f(10 + k, 0, away, (sec, away_x, k)))
            for k, y in enumerate((0, GY - 1)):
                act(copy_f(18 + k, 1, away, (other, away_x, y)))

    each_send(lambda copy: copy.start())
    frac[0, home] = cf[...]
    for slot in range(SLOTS):

        @pl.when(slot != home)
        def _():
            copy_f(0, 0, slot, (sec, gx, lax.rem(gy + 1, GY))).wait_recv()

    @pl.when(at_end)
    def _():
        for slot in range(SLOTS):
            copy_f(0, 1, slot, (sec, gx, lax.rem(gy + 1, GY))).wait_recv()

    shift = lax.rem(COARSE + HALF - 32 * gy, COARSE)
    rows = SLOTS * 8
    mine = pltpu.roll(frac[0].reshape(rows, COARSE), shift, 1)[:, :TILE]
    beyond = pltpu.roll(frac[1].reshape(rows, COARSE), shift, 1)[:, :TILE]
    place = lanes((rows, TILE))
    from_other = ((place < HALF) & (gy == 0)) | ((place >= HALF + 32) & (gy == GY - 1))
    window = jnp.where(from_other, beyond, mine)
    j, i = sublanes((TILE, 32)), lanes((TILE, 32))
    band_y = ((j >= i) & (j < i + WIN)).astype(F32)
    i, m = sublanes((64, rows)), lanes((64, rows))
    which, i = i // 32, lax.rem(i, 32)
    at_row = (m // 8) * 4 + lax.rem(m, 4)
    band_x = ((lax.rem(m, 8) // 4 == which) & (at_row >= i) & (at_row < i + WIN)).astype(F32)
    sums = jnp.dot(window, band_y, precision=lax.Precision.HIGHEST, preferred_element_type=F32)
    area = jnp.dot(band_x, sums, precision=lax.Precision.HIGHEST, preferred_element_type=F32)
    area = area * (1.0 / (WIN * WIN))
    own = pltpu.roll(window, TILE - HALF, 1)
    for c in range(2):
        area_out[c] = area[32 * c : 32 * c + 32, :]
        for k in range(GY):
            at = 8 * (k + 3) + 4 * c
            column_out[c, 4 * k : 4 * k + 4, :] = own[at : at + 4, 0:32]

    for side in range(2):
        for f in range(FIELDS):
            copy_x(side, f).wait_send()
    for k in range(3):
        copy_p(k).wait_send()
    for k in range(1, GY):
        copy_l(k).wait_send()
    each_send(lambda copy: copy.wait_send())


def write_out(adv, column_fraction, area_fraction, out, column_out, area_out, sem):
    copies = [
        pltpu.make_async_copy(adv.at[f], out.at[f], sem.at[f]) for f in range(FIELDS)
    ] + [
        pltpu.make_async_copy(column_fraction, column_out, sem.at[FIELDS]),
        pltpu.make_async_copy(area_fraction, area_out, sem.at[FIELDS + 1]),
    ]
    for copy in copies:
        copy.start()
    for copy in copies:
        copy.wait()


def on_device(
    state, h_coeff, v_coeff, conv_weight, conv_bias, readout, readout_bias, level_base, level_depth
):
    vmem = pl.BlockSpec(memory_space=pltpu.VMEM)
    smem = pl.BlockSpec(memory_space=pltpu.SMEM)
    anywhere = pl.BlockSpec(memory_space=pl.ANY)
    dma = pltpu.SemaphoreType.DMA
    taps = KERNEL * KERNEL
    out, column_fraction, area_fraction = pl.pallas_call(
        kernel,
        out_shape=(
            pltpu.VMEM((FIELDS, ROWS, LEV, COLS), F32),
            pltpu.VMEM((2, 32, 32), F32),
            pltpu.VMEM((2, 32, 32), F32),
        ),
        in_specs=[anywhere, vmem, vmem, vmem, smem, smem, smem, vmem, vmem],
        out_specs=(vmem, vmem, vmem),
        scratch_shapes=[
            pltpu.VMEM((FIELDS, ROWS + 8, LEV, WIDE), F32),
            pltpu.VMEM((FIELDS, ROWS + 4, LEV, WIDE), F32),
            pltpu.VMEM((FIELDS, ROWS, LEV, COLS), BF16),
            pltpu.VMEM((FIELDS, 3, LEV, TILE), F32),
            pltpu.VMEM((2 * TILE, 2 * TILE), BF16),
            pltpu.VMEM((2, FIELDS, 4, LEV, COLS), BF16),
            pltpu.VMEM((2, FIELDS, 4, LEV, COLS), BF16),
            pltpu.VMEM((5, LEV, TILE), F32),
            pltpu.VMEM((7, LEV, TILE), F32),
            pltpu.VMEM((GY, 2, 8, TILE), F32),
            pltpu.VMEM((GY, 2, 8, TILE), F32),
            pltpu.VMEM((KERNEL * TILE, KERNEL * TILE), BF16),
            pltpu.VMEM((taps * FIELDS, CHANNELS), F32),
            pltpu.VMEM((CHANNELS * LEV, FIELDS * taps * LEV), BF16),
            pltpu.VMEM((2, 2, FIELDS * taps * LEV, COARSE), BF16),
            pltpu.VMEM((4, CHANNELS * LEV, COARSE), F32),
            pltpu.VMEM((8, COARSE), F32),
            pltpu.VMEM((2, SLOTS, 8, COARSE), F32),
            dma((3, FIELDS)),
            dma((2, FIELDS)),
            dma((2, FIELDS)),
            dma((3,)),
            dma((3,)),
            dma((GY,)),
            dma((GY,)),
            dma((20,)),
            dma((2, SLOTS)),
        ],
        compiler_params=pltpu.CompilerParams(
            collective_id=0, has_side_effects=True, vmem_limit_bytes=48 * 2**20
        ),
        name="steps_and_fractions",
    )(
        jnp.transpose(state, (0, 2, 1, 3)),
        h_coeff,
        v_coeff,
        jnp.transpose(conv_weight, (1, 2, 0, 3)),
        conv_bias,
        jnp.transpose(readout),
        readout_bias,
        level_base,
        level_depth,
    )
    out, column_fraction, area_fraction = pl.pallas_call(
        write_out,
        out_shape=(
            jax.ShapeDtypeStruct((FIELDS, ROWS, LEV, COLS), F32),
            jax.ShapeDtypeStruct((2, 32, 32), F32),
            jax.ShapeDtypeStruct((2, 32, 32), F32),
        ),
        in_specs=[vmem, vmem, vmem],
        out_specs=(anywhere, anywhere, anywhere),
        scratch_shapes=[dma((FIELDS + 2,))],
        compiler_params=pltpu.CompilerParams(vmem_limit_bytes=2**20),
        name="write_out",
    )(out, column_fraction, area_fraction)
    return jnp.transpose(out, (0, 2, 1, 3)), column_fraction, area_fraction


def solution(mesh):
    in_specs = (
        P(None, None, ("gx", "gy"), "sec"),
        P(),
        P(),
        P(),
        P(),
        P(),
        P(),
        P(None, "gx", ("sec", "gy")),
        P(None, "gx", ("sec", "gy")),
    )
    out_specs = (
        P(None, None, ("gx", "gy"), "sec"),
        P(None, "gx", ("sec", "gy")),
        P(None, "gx", ("sec", "gy")),
    )
    return jax.shard_map(
        on_device, mesh=mesh, in_specs=in_specs, out_specs=out_specs, check_vma=False
    )
```
